512 devices in a mesh: head: 8 (over x, core), seq: 64 (over y, z).
Axes of the slice: x: 4, y: 4, z: 16, core: 2. Of those that a mesh axis runs over, the one named last changes fastest.
Arguments:
- queries: bfloat16 [32768, 4096], P('seq', 'head'), may hold values from -6 to 6
- keys: bfloat16 [32768, 4096], P('seq', 'head'), may hold values from -6 to 6
- values: bfloat16 [32768, 4096], P('seq', 'head'), may hold values from -6 to 6
- out_grad: bfloat16 [32768, 4096], P('seq', 'head'), may hold values from -8 to 8
- inputs: bfloat16 [32768, 2048], P('seq'), may hold values from -100 to 100
- momentum: float32 [2048, 4096], P('seq', 'head'), may hold values from -6 to 6
- level_weight: int32 [18, 32], replicated, may hold values from 1 to 8
Outputs:
- query_grad: bfloat16 [32768, 4096], P('seq', 'head')
- key_grad: bfloat16 [32768, 4096], P('seq', 'head')
- value_grad: bfloat16 [32768, 4096], P('seq', 'head')
- new_momentum: float32 [2048, 4096], P('seq', 'head')
The draws below stay inside these ranges and needn't reach their ends.
All inputs are finite; a program needn't handle non-finite values.
Results may differ from the reference program's by a relative error of at most 0.0095.
Values may be sent and summed in bfloat16 or wider, within the bound.
No kernel may reach another device: no remote copies, remote signals or barrier semaphores. Data moves between devices by JAX's collectives and lax.ppermute only.
A program may use at most 64 MiB of HBM per device.

```python
import math
import jax
import jax.numpy as jnp
from jax import lax

TOK_DEV = 512
HEADS = 32
D_HEAD = 128
DX = 2048
LEVELS = 18
TOKENS = 32768
N_SEQ = 64


def draw_inputs(key, part):
    first = jax.random.fold_in(key, 11)
    second = jax.random.fold_in(key, 12)
    third = jax.random.fold_in(key, 13)
    rise = 1.0 + 2.0 * jnp.arange(DX, dtype=jnp.float32) / DX
    spread = jnp.exp(jax.random.uniform(first, (DX,), jnp.float32) * jnp.log(10.0))
    rowscale = jnp.exp(jax.random.uniform(second, (TOKENS, 1), jnp.float32) * jnp.log(10.0)) / 3.0
    noise = jax.random.truncated_normal(third, -4.0, 4.0, (TOKENS, DX), jnp.float32)
    return (noise * rowscale * rise * spread / 4.0).astype(jnp.bfloat16)


def draw_out_grad(key, part):
    first = jax.random.fold_in(key, 21)
    width = HEADS * D_HEAD
    head_of = (jnp.arange(width, dtype=jnp.int32) // D_HEAD).astype(jnp.float32)
    rise = 1.0 + head_of / max(HEADS - 1, 1)
    noise = jax.random.truncated_normal(first, -4.0, 4.0, (TOKENS, width), jnp.float32)
    return (noise * rise).astype(jnp.bfloat16)


def place_ends(result, rng, least, top_value):
    longest = result.shape.index(max(result.shape))
    spots = []
    for shift in (0, 1):
        where = [jax.random.randint(jax.random.fold_in(rng, axis), (), 0, length) for axis, length in enumerate(result.shape)]
        where[longest] = (where[longest] + shift) % result.shape[longest]
        spots.append(tuple(where))
    return result.at[spots[0]].set(least).at[spots[1]].set(top_value)


def shard_levels(stream_key, dims, split, least, high):
    gain, own = 1.0, jax.random.fold_in(stream_key, 6)
    for position, shards_of in split:
        steps = jnp.exp(jax.random.uniform(jax.random.fold_in(own, position), (shards_of,), jnp.float32, least / len(split), high / len(split)))
        gain = gain * jnp.repeat(steps, dims[position] // shards_of).reshape([-1 if axis == position else 1 for axis in range(len(dims))])
    return gain


def bell_draw(key, extent, scale, reach, shards=(), kind=jnp.bfloat16):
    entries = jax.random.normal(key, extent, jnp.float32) * scale
    if len(shards) > 0:
        entries = shard_levels(key, extent, shards, -0.22, 0.18) * entries
    return jnp.clip(entries, min=-reach, max=reach).astype(kind)


def setup_inputs(seed: int = 0) -> dict:
    splits = jax.random.split(jax.random.key(seed), 8)
    return {
        "queries": bell_draw(splits[0], (TOKENS, HEADS * D_HEAD), 1.0, 6.0, ((0, 64), (1, 8))),
        "keys": bell_draw(splits[1], (TOKENS, HEADS * D_HEAD), 1.0, 6.0, ((0, 64), (1, 8))),
        "values": bell_draw(splits[2], (TOKENS, HEADS * D_HEAD), 1.0, 6.0, ((0, 64), (1, 8))),
        "out_grad": draw_out_grad(jax.random.fold_in(splits[7], 71), 0),
        "inputs": draw_inputs(jax.random.fold_in(splits[7], 71), 0),
        "momentum": bell_draw(splits[5], (DX, HEADS * D_HEAD), 1.0, 6.0, ((0, 64), (1, 8)), jnp.float32),
        "level_weight": place_ends(jax.random.randint(splits[6], (LEVELS, HEADS), 1, 9), jax.random.fold_in(splits[6], 1), 1, 8).astype(jnp.int32),
    }


clip_norm = 1024.0
momentum_rate = 0.9

def bit_length(numbers, count):
    total = jnp.zeros_like(numbers)
    for place in range(count):
        total = total + (jnp.right_shift(numbers, place) > 0).astype(jnp.int32)
    return total

def level_table(level_weight, head_size):
    levels = jnp.arange(level_weight.shape[0], dtype=jnp.float32)
    factor = jnp.exp2(-0.5 * levels) / (8.0 * math.sqrt(head_size))
    return level_weight.astype(jnp.float32) * factor[:, None]

def lookup(level, table):
    onehot = (level[..., None] == jnp.arange(table.shape[0], dtype=jnp.int32)).astype(jnp.float32)
    flat = onehot.reshape(-1, table.shape[0])
    picked = jnp.dot(flat, table, precision=lax.Precision.HIGHEST)
    return picked.reshape(level.shape + (table.shape[1],))

def intra_weights(length, table):
    place = jnp.arange(length, dtype=jnp.int32)
    level = bit_length(jnp.bitwise_xor(place[:, None], place[None, :]), table.shape[0])
    picked = lookup(level, table)
    causal = (place[None, :] <= place[:, None])[..., None]
    return jnp.transpose(jnp.where(causal, picked, jnp.float32(0.0)), (2, 0, 1))

def span_grads(pieces, weights):
    query, key_rows, value_rows, grad_rows = [piece.astype(jnp.float32) for piece in pieces]
    scores = jnp.einsum('thd,shd->hts', query, key_rows)
    mixed = lax.optimization_barrier((weights * scores).astype(jnp.bfloat16)).astype(jnp.float32)
    value_part = jnp.einsum('hts,thd->shd', mixed, grad_rows)
    before = jnp.einsum('thd,shd->hts', grad_rows, value_rows)
    dmix = lax.optimization_barrier((weights * before).astype(jnp.bfloat16)).astype(jnp.float32)
    query_part = jnp.einsum('hts,shd->thd', dmix, key_rows)
    key_part = jnp.einsum('hts,thd->shd', dmix, query)
    return (query_part, key_part, value_part)

def reference(queries, keys, values, out_grad, inputs, momentum, level_weight):
    table = level_table(level_weight, D_HEAD)
    base_level = TOK_DEV.bit_length() - 1
    shape = (N_SEQ, TOK_DEV, HEADS, D_HEAD)
    query = queries.reshape(shape)
    key_rows = keys.reshape(shape)
    value_rows = values.reshape(shape)
    grad_rows = out_grad.reshape(shape)
    weights = intra_weights(TOK_DEV, table)

    def one_span(pieces):
        return span_grads(pieces, weights)
    query_part, key_part, value_part = lax.map(one_span, (query, key_rows, value_rows, grad_rows))
    key32 = key_rows.astype(jnp.float32)
    value32 = value_rows.astype(jnp.float32)
    query32 = query.astype(jnp.float32)
    grad32 = grad_rows.astype(jnp.float32)
    states = jnp.einsum('cthd,cthe->chde', key32, value32).astype(jnp.bfloat16)
    grads = jnp.einsum('cthd,cthe->chde', query32, grad32).astype(jnp.bfloat16)
    span = jnp.arange(N_SEQ, dtype=jnp.int32)
    level = bit_length(jnp.bitwise_xor(span[:, None], span[None, :]), table.shape[0]) + base_level
    across = jnp.where((span[None, :] < span[:, None])[..., None], lookup(level, table), jnp.float32(0.0))
    carried = jnp.einsum('ijh,jhde->ihde', across, states.astype(jnp.float32), precision=lax.Precision.HIGHEST).astype(jnp.bfloat16)
    returned = jnp.einsum('ijh,ihde->jhde', across, grads.astype(jnp.float32), precision=lax.Precision.HIGHEST).astype(jnp.bfloat16)
    carried32 = carried.astype(jnp.float32)
    returned32 = returned.astype(jnp.float32)
    width = HEADS * D_HEAD
    query_grad = (query_part + jnp.einsum('cthe,chde->cthd', grad32, carried32)).astype(jnp.bfloat16).reshape(TOKENS, width)
    key_grad = (key_part + jnp.einsum('cthe,chde->cthd', value32, returned32)).astype(jnp.bfloat16).reshape(TOKENS, width)
    value_grad = (value_part + jnp.einsum('cthd,chde->cthe', key32, returned32)).astype(jnp.bfloat16).reshape(TOKENS, width)
    proj_grad = jnp.dot(inputs.astype(jnp.float32).T, value_grad.astype(jnp.float32), precision=lax.Precision.HIGHEST, preferred_element_type=jnp.float32)
    norm = jnp.sqrt(jnp.sum(proj_grad * proj_grad) + 1e-06)
    factor = jnp.minimum(jnp.float32(1.0), clip_norm / norm)
    new_momentum = momentum_rate * momentum + factor * proj_grad
    return (query_grad, key_grad, value_grad, new_momentum)
```

```python
import functools
import math

import jax
import jax.numpy as jnp
import numpy as np
from jax import lax
from jax.experimental import pallas as pl
from jax.experimental.pallas import tpu as pltpu
from jax.sharding import Mesh
from jax.sharding import PartitionSpec as P

D = 128
HEAD = ("head_0", "head_1")
Y = "seq_0"
Z = "seq_1"
SEQ = (Y, Z)

clip_norm = 1024.0
momentum_rate = 0.9

bf16 = jnp.bfloat16
f32 = jnp.float32

SMEM = pl.BlockSpec(memory_space=pltpu.SMEM)
VMEM = pl.BlockSpec(memory_space=pltpu.VMEM)


def dot(a, b, ca, cb):
    return lax.dot_general(a, b, (((ca,), (cb,)), ((), ())), preferred_element_type=f32)


def call(kernel, out_shape, operands, flops, scratch=(), vmem=16, scalars=0, after=()):
    n = len(operands)

    def run(*refs):
        kernel(*refs[:n], *refs[n + len(after) :])

    leaves = jax.tree.leaves((operands, out_shape))
    return pl.pallas_call(
        run,
        out_shape=out_shape,
        in_specs=[SMEM] * scalars
        + [VMEM] * (n - scalars)
        + [pl.BlockSpec(memory_space=pl.ANY)] * len(after),
        out_specs=jax.tree.map(lambda _: VMEM, out_shape),
        scratch_shapes=list(scratch),
        compiler_params=pltpu.CompilerParams(vmem_limit_bytes=vmem * 1024 * 1024),
        cost_estimate=pl.CostEstimate(
            flops=flops,
            bytes_accessed=sum(x.size * x.dtype.itemsize for x in leaves),
            transcendentals=0,
        ),
    )(*operands, *after)


def lanes(block):
    if isinstance(block, int):
        return slice(block * D, (block + 1) * D)
    return pl.ds(pl.multiple_of(block * D, D), D)


def lam(level, head, weight_ref):
    factor = np.float32(2.0 ** (-0.5 * level) / (8.0 * math.sqrt(D)))
    return weight_ref[level, head].astype(f32) * factor


def diagonal(head, weight_ref, transposed):
    row = lax.broadcasted_iota(jnp.int32, (D, D), 0)
    col = lax.broadcasted_iota(jnp.int32, (D, D), 1)
    apart = jnp.bitwise_xor(row, col)
    out = jnp.full((D, D), lam(0, head, weight_ref), f32)
    for level in range(1, D.bit_length()):
        out = jnp.where(apart >= 1 << (level - 1), lam(level, head, weight_ref), out)
    keep = row <= col if transposed else col <= row
    return jnp.where(keep, out, f32(0.0))


def far(i, j, head, weight_ref):
    return lam(D.bit_length() - 1 + (i ^ j).bit_length(), head, weight_ref)


def weighted(scores, first, own, head, weight_ref, diag):
    count = scores.shape[1] // D
    parts = []
    for n in range(count):
        part = scores[:, n * D : (n + 1) * D]
        w = diag if first + n == own else far(first + n, own, head, weight_ref)
        parts.append((w * part).astype(bf16))
    return parts[0] if count == 1 else jnp.concatenate(parts, axis=1)


def states_kernel(q_ref, k_ref, v_ref, g_ref, out_ref):
    for h in range(out_ref.shape[0]):
        s = lanes(h)
        out_ref[h, :D, :] = dot(q_ref[:, s], g_ref[:, s], 0, 0).astype(bf16)
        out_ref[h, D:, :] = dot(k_ref[:, s], v_ref[:, s], 0, 0).astype(bf16)


def keyed_kernel(info_ref, x_ref, k_ref, *out_refs):
    y = info_ref[1]
    n_out = len(out_refs)
    heads = [lanes(lax.rem(y + n, n_out)) for n in range(n_out)]
    keys = jnp.concatenate([k_ref[:, s] for s in heads], axis=1)
    width = 512
    for c in range(x_ref.shape[1] // width):
        part = slice(c * width, (c + 1) * width)
        res = dot(x_ref[:, part], keys, 0, 0).astype(bf16)
        for n in range(n_out):
            out_refs[n][part, :] = res[:, lanes(n)]


def local_kernel(info_ref, weight_ref, q_ref, k_ref, g_ref, x_ref, loc_ref, proj_ref, low_ref):
    heads = proj_ref.shape[0]
    blocks = q_ref.shape[0] // D
    for h in range(heads):
        s = lanes(h)
        head = info_ref[0] * heads + h
        diag = diagonal(head, weight_ref, True)
        for j in range(blocks):
            rows = slice(j * D, (j + 1) * D)
            scores = dot(k_ref[rows, s], q_ref[j * D :, s], 1, 1)
            mixed = weighted(scores, j, j, head, weight_ref, diag)
            res = dot(mixed, g_ref[j * D :, s], 1, 0)
            loc_ref[rows, s] = res
            low_ref[rows, s] = res.astype(bf16)
    width = 512
    for c in range(x_ref.shape[1] // width):
        part = slice(c * width, (c + 1) * width)
        res = dot(x_ref[:, part], low_ref[...], 0, 0).astype(bf16)
        for h in range(heads):
            proj_ref[h, part, :] = res[:, lanes(h)]


def tree_kernel(info_ref, weight_ref, in_ref, out_ref):
    nz, ny = in_ref.shape[:2]
    count = nz * ny
    depth = count.bit_length() - 1
    head = info_ref[0] * ny + info_ref[1]
    is_grad = info_ref[2] < nz // 2
    sums = [[in_ref[c % nz, c // nz].astype(f32) for c in range(count)]]
    for bit in range(depth - 1):
        last = sums[-1]
        sums.append([last[2 * b] + last[2 * b + 1] for b in range(len(last) // 2)])
    total = [jnp.zeros(in_ref.shape[2:], f32)]
    for bit in reversed(range(depth)):
        w = lam(D.bit_length() + 2 + bit, head, weight_ref)
        later = jnp.where(is_grad, w, f32(0.0))
        earlier = jnp.where(is_grad, f32(0.0), w)
        last = sums[bit]
        total = [
            total[b // 2] + (later * last[b + 1] if b % 2 == 0 else earlier * last[b - 1])
            for b in range(len(last))
        ]
    for c in range(count):
        out_ref[c % nz, c // nz] = total[c].astype(bf16)


def project_kernel(info_ref, a0, a1, a2, a3, loc_ref, r_ref, out_ref, *own_refs):
    y = info_ref[1]
    keyed = (a0, a1, a2, a3)
    n_y = len(keyed)
    half = r_ref.shape[0] // 2
    nz = out_ref.shape[0]
    each = out_ref.shape[1] // n_y
    states = []
    for n in range(n_y):
        states.append(r_ref[:half, lax.rem(y + n_y - n, n_y)].reshape(D, D))
        own_refs[n][...] = r_ref[:, lax.rem(y + n, n_y)].reshape(2 * D, D)
    rows = nz * each
    both = [jnp.concatenate(states[i : i + 2], axis=0) for i in range(0, n_y, 2)]
    for b in range(n_y):
        part = slice(b * rows, (b + 1) * rows)
        res = loc_ref[part, :].astype(f32)
        for i in range(0, n_y, 2):
            left = jnp.concatenate([keyed[i][part, :], keyed[i + 1][part, :]], axis=1)
            res = res + dot(left, both[i // 2], 1, 0)
        res = res.astype(bf16)
        for z in range(nz):
            out_ref[z, b * each : (b + 1) * each, :] = res[z * each : (z + 1) * each, :]


def outputs_kernel(
    info_ref, weight_ref, q_ref, k_ref, v_ref, g_ref, loc_ref, r0, r1, r2, r3, dq_ref, dk_ref, dv_ref
):
    y = info_ref[1]
    states = (r0, r1, r2, r3)
    n_y = len(states)
    blocks = q_ref.shape[0] // D
    for n in range(n_y):
        h = lax.rem(y + n_y - n, n_y)
        s = lanes(h)
        head = info_ref[0] * n_y + h
        returned = states[n][:D, :]
        carried = states[n][D:, :]
        query, keys, values, grad = q_ref[:, s], k_ref[:, s], v_ref[:, s], g_ref[:, s]
        dv_ref[:, s] = (loc_ref[:, s] + dot(keys, returned, 1, 0)).astype(bf16)
        base_k = dot(values, returned, 1, 1)
        base_q = dot(grad, carried, 1, 1)
        diag = diagonal(head, weight_ref, False)
        diag_t = diagonal(head, weight_ref, True)
        for i in range(blocks):
            rows = slice(i * D, (i + 1) * D)
            upto = (i + 1) * D
            before = dot(grad[rows], values[:upto], 1, 1)
            dmix = weighted(before, 0, i, head, weight_ref, diag)
            dq_ref[rows, s] = (base_q[rows] + dot(dmix, keys[:upto], 1, 0)).astype(bf16)
            after = dot(values[rows], grad[i * D :], 1, 1)
            dmix_t = weighted(after, i, i, head, weight_ref, diag_t)
            dk_ref[rows, s] = (base_k[rows] + dot(dmix_t, query[i * D :], 1, 0)).astype(bf16)


def shard_kernel(in_ref, out_ref):
    n_y, rows = out_ref.shape[0], out_ref.shape[1] - 8
    total = in_ref[0].astype(f32)
    for z in range(1, in_ref.shape[0]):
        total = total + in_ref[z].astype(f32)
    square = jnp.sum(jnp.sum(total * total, axis=0, keepdims=True), axis=1, keepdims=True)
    for b in range(n_y):
        out_ref[b, :rows, :] = total[b * rows : (b + 1) * rows, :]
        out_ref[b, rows:, :] = jnp.broadcast_to(square, (8, D))


def final_kernel(mom_ref, in_ref, total_ref, out_ref):
    rows = mom_ref.shape[0]
    total = jnp.sum(total_ref[...], axis=0)
    factor = jnp.minimum(f32(1.0), clip_norm / jnp.sqrt(total + 1e-06))
    for h in range(in_ref.shape[0]):
        s = lanes(h)
        out_ref[:, s] = momentum_rate * mom_ref[:, s] + factor * in_ref[h, :rows, :]


def shift(x, axis, by):
    n = lax.axis_size(axis)
    return lax.ppermute(x, axis, [(i, (i + by) % n) for i in range(n)])


def swap(x, axes):
    return lax.all_to_all(x, axes, 0, 0, tiled=True)


def body(queries, keys, values, out_grad, inputs, momentum, level_weight):
    length, width = queries.shape
    features = inputs.shape[1]
    n_y, n_z = lax.axis_size(Y), lax.axis_size(Z)
    heads = width // D
    sds = jax.ShapeDtypeStruct
    info = jnp.stack(
        [lax.axis_index(HEAD), lax.axis_index(Y), lax.axis_index(Z), jnp.int32(0)]
    ).astype(jnp.int32)

    both = call(
        states_kernel,
        sds((heads, 2 * D, D), bf16),
        (queries, keys, values, out_grad),
        4 * length * width * D,
    )
    keyed = call(
        keyed_kernel,
        tuple(sds((features, D), bf16) for _ in range(n_y)),
        (info, inputs, keys),
        2 * length * width * features,
        scalars=1,
        after=(both,),
    )
    both = swap(both, Y)
    both = both.reshape(n_y, n_z, 2 * D // n_z, D).transpose(1, 0, 2, 3)

    local, proj = call(
        local_kernel,
        (sds((length, width), f32), sds((heads, features, D), bf16)),
        (info, level_weight, queries, keys, out_grad, inputs),
        2 * length * width * features + 3 * length * length * width,
        [pltpu.VMEM((length, width), bf16)],
        scalars=2,
        after=(keyed[0], both),
    )
    both = swap(both, Z)
    keyed = [keyed[0]] + [shift(keyed[n], Y, n) for n in range(1, n_y)]
    proj = lax.psum_scatter(
        proj.reshape(heads * features, D), Y, scatter_dimension=0, tiled=True
    )

    both = call(
        tree_kernel,
        sds(both.shape, bf16),
        (info, level_weight, both),
        1 << 21,
        vmem=8,
        scalars=2,
        after=(local,),
    )
    both = swap(both, Z)

    parts, *own = call(
        project_kernel,
        (sds((n_z, features // n_z, D), bf16),) + tuple(sds((2 * D, D), bf16) for _ in range(n_y)),
        (info, *keyed, proj, both),
        2 * features * n_y * D * D,
        scalars=1,
    )
    parts = swap(parts, Z)

    own = [own[0]] + [shift(own[n], Y, n) for n in range(1, n_y)]
    query_grad, key_grad, value_grad = call(
        outputs_kernel,
        tuple(sds((length, width), bf16) for _ in range(3)),
        (info, level_weight, queries, keys, values, out_grad, local, *own),
        6 * length * length * width,
        scalars=2,
    )

    rows = momentum.shape[0]
    shard = call(
        shard_kernel,
        sds((n_y, rows + 8, D), f32),
        (parts,),
        1 << 20,
        vmem=8,
        after=(query_grad,),
    )
    shard = swap(shard, Y)
    rest = HEAD + (Z,)
    square = jnp.sum(shard[:, rows : rows + 1, :], axis=0, keepdims=True)
    total = swap(jnp.broadcast_to(square, (lax.axis_size(rest), 1, D)), rest)
    new_momentum = call(
        final_kernel, sds(momentum.shape, f32), (momentum, shard, total), 1 << 16, vmem=4
    )
    return (query_grad, key_grad, value_grad, new_momentum)


def solution(mesh):
    torus = Mesh(mesh.devices.reshape(4, 2, 4, 16), HEAD + SEQ)
    tokens = P(SEQ, HEAD)
    return jax.shard_map(
        body,
        mesh=torus,
        in_specs=(tokens, tokens, tokens, tokens, P(SEQ, None), tokens, P()),
        out_specs=(tokens, tokens, tokens, tokens),
        check_vma=False,
    )
```

```python
import functools
import math

import jax
import jax.numpy as jnp
import numpy as np
from jax import lax
from jax.experimental import pallas as pl
from jax.experimental.pallas import tpu as pltpu
from jax.sharding import Mesh
from jax.sharding import PartitionSpec as P

D = 128
HEAD = ("head_0", "head_1")
Y = "seq_0"
Z = "seq_1"
SEQ = (Y, Z)

clip_norm = 1024.0
momentum_rate = 0.9

bf16 = jnp.bfloat16
f32 = jnp.float32


def dot(a, b, ca, cb):
    return lax.dot_general(a, b, (((ca,), (cb,)), ((), ())), preferred_element_type=f32)


def spec(block, index):
    return pl.BlockSpec(block, index)


def call(kernel, out_shape, operands, flops, in_specs=None, out_specs=None, grid=(1,), scratch=(), vmem=60, after=(), scalars=(), gated=()):
    leaves = jax.tree.leaves((operands, out_shape))
    n = len(scalars) + len(operands)
    skip = n + len(after) + len(gated)
    last = skip + len(jax.tree.leaves(out_shape))

    def run(*refs):
        kernel(*refs[:n], *refs[skip:last], *refs[last + len(gated) :])

    def whole(x):
        return spec(x.shape, lambda *_: (0,) * len(x.shape))

    in_specs = list(in_specs or [None] * len(operands))
    in_specs = [whole(x) if i is None else i for x, i in zip(operands, in_specs)]
    if out_specs is None:
        out_specs = jax.tree.map(whole, out_shape)
    anywhere = pl.BlockSpec(memory_space=pl.ANY)
    aliases = {}
    if gated:
        first = len(jax.tree.leaves(out_shape))
        aliases = {n + len(after) + i: first + i for i in range(len(gated))}
        out_shape = (*jax.tree.leaves(out_shape), *(jax.ShapeDtypeStruct(x.shape, x.dtype) for x in gated))
        out_specs = (*jax.tree.leaves(out_specs), *(anywhere for _ in gated))
    return pl.pallas_call(
        run,
        out_shape=out_shape,
        grid_spec=pltpu.PrefetchScalarGridSpec(
            num_scalar_prefetch=len(scalars),
            grid=grid,
            in_specs=in_specs + [anywhere] * (len(after) + len(gated)),
            out_specs=out_specs,
            scratch_shapes=list(scratch),
        ),
        input_output_aliases=aliases,
        compiler_params=pltpu.CompilerParams(vmem_limit_bytes=vmem * 1024 * 1024),
        cost_estimate=pl.CostEstimate(
            flops=flops,
            bytes_accessed=sum(x.size * x.dtype.itemsize for x in leaves),
            transcendentals=0,
        ),
    )(*scalars, *operands, *after, *gated)


def lanes(block):
    if isinstance(block, int):
        return slice(block * D, (block + 1) * D)
    return pl.ds(pl.multiple_of(block * D, D), D)


def lam(level, head, weight_ref):
    factor = np.float32(2.0 ** (-0.5 * level) / (8.0 * math.sqrt(D)))
    return weight_ref[level, head].astype(f32) * factor


def diagonal(head, weight_ref, transposed):
    row = lax.broadcasted_iota(jnp.int32, (D, D), 0)
    col = lax.broadcasted_iota(jnp.int32, (D, D), 1)
    apart = jnp.bitwise_xor(row, col)
    out = jnp.full((D, D), lam(0, head, weight_ref), f32)
    for level in range(1, D.bit_length()):
        out = jnp.where(apart >= 1 << (level - 1), lam(level, head, weight_ref), out)
    keep = row <= col if transposed else col <= row
    return jnp.where(keep, out, f32(0.0))


def far(i, j, head, weight_ref):
    return lam(D.bit_length() - 1 + (i ^ j).bit_length(), head, weight_ref)


def weighted(scores, first, own, head, weight_ref, diag):
    count = scores.shape[1] // D
    parts = []
    for n in range(count):
        part = scores[:, n * D : (n + 1) * D]
        w = diag if first + n == own else far(first + n, own, head, weight_ref)
        parts.append((w * part).astype(bf16))
    return parts[0] if count == 1 else jnp.concatenate(parts, axis=1)


def states_kernel(q_ref, k_ref, v_ref, g_ref, out_ref):
    out_ref[0, :D, :] = dot(q_ref[...], g_ref[...], 0, 0).astype(bf16)
    out_ref[0, D:, :] = dot(k_ref[...], v_ref[...], 0, 0).astype(bf16)


def local_kernel(info_ref, weight_ref, q_ref, k_ref, g_ref, out_ref):
    blocks = q_ref.shape[0] // D
    head = info_ref[0] * pl.num_programs(0) + pl.program_id(0)
    diag = diagonal(head, weight_ref, True)
    for j in range(blocks):
        rows = slice(j * D, (j + 1) * D)
        scores = dot(k_ref[rows, :], q_ref[j * D :, :], 1, 1)
        mixed = weighted(scores, j, j, head, weight_ref, diag)
        out_ref[rows, :] = dot(mixed, g_ref[j * D :, :], 1, 0)


def keyed_kernel(info_ref, x_ref, k_ref, loc_ref, proj_ref, *out_refs):
    y = info_ref[1]
    n_out = len(out_refs)
    heads = [lanes(lax.rem(y + n, n_out)) for n in range(n_out)]
    right = jnp.concatenate([k_ref[:, s] for s in heads] + [loc_ref[...].astype(bf16)], axis=1)
    res = dot(x_ref[...], right, 0, 0).astype(bf16)
    for n in range(n_out):
        out_refs[n][...] = res[:, lanes(n)]
        proj_ref[n, :, :] = res[:, lanes(n_out + n)]


def turn_kernel(in_ref, out_ref):
    each = out_ref.shape[2]
    for z in range(out_ref.shape[0]):
        for y in range(out_ref.shape[1]):
            out_ref[z, y, :, :] = in_ref[y, z * each : (z + 1) * each, :]


def tree_kernel(info_ref, weight_ref, in_ref, out_ref):
    nz, ny = in_ref.shape[:2]
    count = nz * ny
    depth = count.bit_length() - 1
    head = info_ref[0] * ny + info_ref[1]
    is_grad = info_ref[2] < nz // 2
    sums = [[in_ref[c % nz, c // nz].astype(f32) for c in range(count)]]
    for bit in range(depth - 1):
        last = sums[-1]
        sums.append([last[2 * b] + last[2 * b + 1] for b in range(len(last) // 2)])
    total = [jnp.zeros(in_ref.shape[2:], f32)]
    for bit in reversed(range(depth)):
        w = lam(D.bit_length() + 2 + bit, head, weight_ref)
        later = jnp.where(is_grad, w, f32(0.0))
        earlier = jnp.where(is_grad, f32(0.0), w)
        last = sums[bit]
        total = [
            total[b // 2] + (later * last[b + 1] if b % 2 == 0 else earlier * last[b - 1])
            for b in range(len(last))
        ]
    for c in range(count):
        out_ref[c % nz, c // nz] = total[c].astype(bf16)


def project_kernel(info_ref, a0, a1, a2, a3, loc_ref, r_ref, out_ref, *own_refs):
    y = info_ref[1]
    keyed = (a0, a1, a2, a3)
    n_y = len(keyed)
    half = r_ref.shape[0] // 2
    nz, each = out_ref.shape[:2]

    @pl.when(pl.program_id(0) == 0)
    def _():
        for n in range(n_y):
            own_refs[n][...] = r_ref[:, lax.rem(y + n, n_y)].reshape(2 * D, D)

    states = [r_ref[:half, lax.rem(y + n_y - n, n_y)].reshape(D, D) for n in range(n_y)]
    left = jnp.concatenate([a[...] for a in keyed], axis=1)
    res = loc_ref[...].astype(f32) + dot(left, jnp.concatenate(states, axis=0), 1, 0)
    res = res.astype(bf16)
    for z in range(nz):
        out_ref[z, :, :] = res[z * each : (z + 1) * each, :]


def outputs_kernel(
    info_ref, weight_ref, q_ref, k_ref, v_ref, g_ref, loc_ref, r0, r1, r2, r3, dq_ref, dk_ref, dv_ref, r_ref
):
    n = pl.program_id(0)
    n_y = pl.num_programs(0)
    for i, r in enumerate((r0, r1, r2, r3)):

        @pl.when(n == i)
        def _():
            r_ref[...] = r[...]

    blocks = q_ref.shape[0] // D
    head = info_ref[0] * n_y + lax.rem(info_ref[1] + n_y - n, n_y)
    returned = r_ref[:D, :]
    carried = r_ref[D:, :]
    query, keys, values, grad = q_ref[...], k_ref[...], v_ref[...], g_ref[...]
    dv_ref[...] = (loc_ref[...] + dot(keys, returned, 1, 0)).astype(bf16)
    base_k = dot(values, returned, 1, 1)
    base_q = dot(grad, carried, 1, 1)
    diag = diagonal(head, weight_ref, False)
    diag_t = diagonal(head, weight_ref, True)
    for i in range(blocks):
        rows = slice(i * D, (i + 1) * D)
        upto = (i + 1) * D
        before = dot(grad[rows], values[:upto], 1, 1)
        dmix = weighted(before, 0, i, head, weight_ref, diag)
        dq_ref[rows, :] = (base_q[rows] + dot(dmix, keys[:upto], 1, 0)).astype(bf16)
        later = dot(values[rows], grad[i * D :], 1, 1)
        dmix_t = weighted(later, i, i, head, weight_ref, diag_t)
        dk_ref[rows, :] = (base_k[rows] + dot(dmix_t, query[i * D :], 1, 0)).astype(bf16)


def shard_kernel(in_ref, out_ref, square_ref):
    total = in_ref[0].astype(f32)
    for z in range(1, in_ref.shape[0]):
        total = total + in_ref[z].astype(f32)
    out_ref[...] = total
    square = jnp.sum(jnp.sum(total * total, axis=0, keepdims=True), axis=1, keepdims=True)
    square_ref[...] = jnp.broadcast_to(square[None], square_ref.shape)


def stage_kernel(info_ref, square_ref, shard_ref, out_ref, *part_refs):
    n_y = len(part_refs)
    rows = part_refs[0].shape[0]
    square = jnp.sum(square_ref[...], axis=0, keepdims=True)
    out_ref[...] = jnp.broadcast_to(square, out_ref.shape)
    for n in range(n_y):
        first = pl.multiple_of(lax.rem(info_ref[1] + n, n_y) * rows, rows)
        part_refs[n][...] = shard_ref[pl.ds(first, rows), :]


def final_kernel(info_ref, mom_ref, p0, p1, p2, p3, total_ref, out_ref):
    parts = (p0, p1, p2, p3)
    n_y = len(parts)
    total = jnp.sum(total_ref[...], axis=0)
    factor = jnp.minimum(f32(1.0), clip_norm / jnp.sqrt(total + 1e-06))
    for n in range(n_y):
        s = lanes(lax.rem(info_ref[1] + n_y - n, n_y))
        out_ref[:, s] = momentum_rate * mom_ref[:, s] + factor * parts[n][...]


def shift(x, axis, by):
    n = lax.axis_size(axis)
    return lax.ppermute(x, axis, [(i, (i + by) % n) for i in range(n)])


def swap(x, axes):
    return lax.all_to_all(x, axes, 0, 0, tiled=True)


def body(queries, keys, values, out_grad, inputs, momentum, level_weight):
    length, width = queries.shape
    features = inputs.shape[1]
    n_y, n_z = lax.axis_size(Y), lax.axis_size(Z)
    heads = width // D
    sds = jax.ShapeDtypeStruct
    info = jnp.stack(
        [lax.axis_index(HEAD), lax.axis_index(Y), lax.axis_index(Z), jnp.int32(0)]
    ).astype(jnp.int32)

    column = spec((length, D), lambda h, *_: (0, h))
    both = call(
        states_kernel,
        sds((heads, 2 * D, D), bf16),
        (queries, keys, values, out_grad),
        4 * length * width * D,
        [column] * 4,
        spec((1, 2 * D, D), lambda h: (h, 0, 0)),
        (heads,),
    )
    local = call(
        local_kernel,
        sds((length, width), f32),
        (queries, keys, out_grad),
        3 * length * length * width,
        [column] * 3,
        column,
        (heads,),
        scalars=(info, level_weight),
        after=(both,),
    )
    block = 512
    steps = features // block
    proj, *keyed = call(
        keyed_kernel,
        (sds((heads, features, D), bf16),) + tuple(sds((features, D), bf16) for _ in range(n_y)),
        (inputs, keys, local),
        4 * length * width * features,
        [spec((length, block), lambda c, *_: (0, c)), None, None],
        (spec((heads, block, D), lambda c, *_: (0, c, 0)),)
        + (spec((block, D), lambda c, *_: (c, 0)),) * n_y,
        (steps,),
        scalars=(info,),
    )
    both, proj, *keyed[1:] = call(
        turn_kernel,
        sds((n_z, n_y, 2 * D // n_z, D), bf16),
        (swap(both, Y),),
        1 << 16,
        gated=(proj, *keyed[1:]),
    )
    both = swap(both, Z)
    keyed = [keyed[0]] + [shift(keyed[n], Y, n) for n in range(1, n_y)]
    proj = lax.psum_scatter(
        proj.reshape(heads * features, D), Y, scatter_dimension=0, tiled=True
    )

    both = call(
        tree_kernel,
        sds(both.shape, bf16),
        (both,),
        1 << 21,
        scalars=(info, level_weight),
        after=keyed[1:],
        vmem=8,
    )
    both = swap(both, Z)

    row = spec((features // n_y, D), lambda b, *_: (b, 0))
    each = features // n_z // n_y
    parts, *own = call(
        project_kernel,
        (sds((n_z, features // n_z, D), bf16),) + tuple(sds((2 * D, D), bf16) for _ in range(n_y)),
        (*keyed, proj, both),
        2 * features * n_y * D * D,
        [row] * (n_y + 1) + [None],
        (spec((n_z, each, D), lambda b, *_: (0, b, 0)),)
        + (spec((2 * D, D), lambda b, *_: (0, 0)),) * n_y,
        (n_y,),
        scalars=(info,),
    )
    parts = swap(parts, Z)

    own = [own[0]] + [shift(own[n], Y, n) for n in range(1, n_y)]
    turned = spec((length, D), lambda n, info_ref, _: (0, lax.rem(info_ref[1] + n_y - n, n_y)))
    query_grad, key_grad, value_grad = call(
        outputs_kernel,
        tuple(sds((length, width), bf16) for _ in range(3)),
        (queries, keys, values, out_grad, local, *own),
        6 * length * length * width,
        [turned] * 5 + [None] * n_y,
        (turned,) * 3,
        (n_y,),
        [pltpu.VMEM((2 * D, D), bf16)],
        scalars=(info, level_weight),
    )

    near, rest = HEAD + (Y,), (Z,)
    rows = momentum.shape[0]
    shard, square = call(
        shard_kernel,
        (sds((n_y * rows, D), f32), sds((lax.axis_size(near), 1, D), f32)),
        (parts,),
        1 << 20,
        after=(query_grad,),
        vmem=8,
    )
    square = swap(square, near)
    total, *mine = call(
        stage_kernel,
        (sds((lax.axis_size(rest), 1, D), f32),) + tuple(sds((rows, D), f32) for _ in range(n_y)),
        (square, shard),
        1 << 16,
        scalars=(info,),
        vmem=8,
    )
    total = swap(total, rest)
    mine = [mine[0]] + [shift(mine[n], Y, n) for n in range(1, n_y)]
    new_momentum = call(
        final_kernel,
        sds(momentum.shape, f32),
        (momentum, *mine, total),
        1 << 16,
        scalars=(info,),
        vmem=8,
    )
    return (query_grad, key_grad, value_grad, new_momentum)


def solution(mesh):
    torus = Mesh(mesh.devices.reshape(4, 2, 4, 16), HEAD + SEQ)
    tokens = P(SEQ, HEAD)
    return jax.shard_map(
        body,
        mesh=torus,
        in_specs=(tokens, tokens, tokens, tokens, P(SEQ, None), tokens, P()),
        out_specs=(tokens, tokens, tokens, tokens),
        check_vma=False,
    )
```

```python
import functools
import math

import jax
import jax.numpy as jnp
import numpy as np
from jax import lax
from jax.experimental import pallas as pl
from jax.experimental.pallas import tpu as pltpu
from jax.sharding import Mesh
from jax.sharding import PartitionSpec as P

D = 128
HEAD = ("head_0", "head_1")
Y = "seq_0"
Z = "seq_1"
SEQ = (Y, Z)

VMEM_ALL = 60

clip_norm = 1024.0
momentum_rate = 0.9

bf16 = jnp.bfloat16
f32 = jnp.float32


def dot(a, b, ca, cb):
    return lax.dot_general(a, b, (((ca,), (cb,)), ((), ())), preferred_element_type=f32)


VMEM = pl.BlockSpec(memory_space=pltpu.VMEM)
ANY = pl.BlockSpec(memory_space=pl.ANY)


def call(kernel, out_shape, operands, flops, in_specs=None, out_specs=None, grid=(), scratch=(), vmem=16, after=(), scalars=(), gated=()):
    leaves = jax.tree.leaves((operands, out_shape))
    n = len(scalars) + len(operands)
    skip = n + len(after) + len(gated)
    last = skip + len(jax.tree.leaves(out_shape))

    def run(*refs):
        kernel(*refs[:n], *refs[skip:last], *refs[last + len(gated) :])

    in_specs = list(in_specs or [None] * len(operands))
    in_specs = [VMEM if i is None else i for i in in_specs]
    if out_specs is None:
        out_specs = jax.tree.map(lambda _: VMEM, out_shape)
    anywhere = ANY
    aliases = {}
    if gated:
        first = len(jax.tree.leaves(out_shape))
        aliases = {n + len(after) + i: first + i for i in range(len(gated))}
        out_shape = (*jax.tree.leaves(out_shape), *(jax.ShapeDtypeStruct(x.shape, x.dtype) for x in gated))
        out_specs = (*jax.tree.leaves(out_specs), *(anywhere for _ in gated))
    return pl.pallas_call(
        run,
        out_shape=out_shape,
        grid_spec=pltpu.PrefetchScalarGridSpec(
            num_scalar_prefetch=len(scalars),
            grid=grid,
            in_specs=in_specs + [anywhere] * (len(after) + len(gated)),
            out_specs=out_specs,
            scratch_shapes=list(scratch),
        ),
        input_output_aliases=aliases,
        compiler_params=pltpu.CompilerParams(vmem_limit_bytes=vmem * 1024 * 1024),
        cost_estimate=pl.CostEstimate(
            flops=flops,
            bytes_accessed=sum(x.size * x.dtype.itemsize for x in leaves),
            transcendentals=0,
        ),
    )(*scalars, *operands, *after, *gated)


def lanes(block):
    if isinstance(block, int):
        return slice(block * D, (block + 1) * D)
    return pl.ds(pl.multiple_of(block * D, D), D)


def lam(level, head, weight_ref):
    factor = np.float32(2.0 ** (-0.5 * level) / (8.0 * math.sqrt(D)))
    return weight_ref[level, head].astype(f32) * factor


def diagonal(head, weight_ref, transposed):
    row = lax.broadcasted_iota(jnp.int32, (D, D), 0)
    col = lax.broadcasted_iota(jnp.int32, (D, D), 1)
    apart = jnp.bitwise_xor(row, col)
    out = jnp.full((D, D), lam(0, head, weight_ref), f32)
    for level in range(1, D.bit_length()):
        out = jnp.where(apart >= 1 << (level - 1), lam(level, head, weight_ref), out)
    keep = row <= col if transposed else col <= row
    return jnp.where(keep, out, f32(0.0))


def far(i, j, head, weight_ref):
    return lam(D.bit_length() - 1 + (i ^ j).bit_length(), head, weight_ref)


def weighted(scores, first, own, head, weight_ref, diag):
    count = scores.shape[1] // D
    parts = []
    for n in range(count):
        part = scores[:, n * D : (n + 1) * D]
        w = diag if first + n == own else far(first + n, own, head, weight_ref)
        parts.append((w * part).astype(bf16))
    return parts[0] if count == 1 else jnp.concatenate(parts, axis=1)


def start_all(pairs, sems):
    moves = [pltpu.make_async_copy(source, to, sems.at[i]) for i, (source, to) in enumerate(pairs)]
    for move in moves:
        move.start()
    return moves


def states_kernel(q_hbm, g_hbm, k_hbm, v_hbm, out_ref, q_ref, g_ref, k_ref, v_ref, sems):
    moves = start_all(
        [(q_hbm, q_ref), (g_hbm, g_ref), (k_hbm, k_ref), (v_hbm, v_ref)], sems
    )
    moves[0].wait()
    moves[1].wait()
    for h in range(out_ref.shape[0]):
        s = lanes(h)
        out_ref[h, :D, :] = dot(q_ref[:, s], g_ref[:, s], 0, 0).astype(bf16)
    moves[2].wait()
    moves[3].wait()
    for h in range(out_ref.shape[0]):
        s = lanes(h)
        out_ref[h, D:, :] = dot(k_ref[:, s], v_ref[:, s], 0, 0).astype(bf16)


def local_kernel(info_ref, weight_ref, q_hbm, k_hbm, g_hbm, x_hbm, loc_ref, proj_hbm, *refs):
    keyed_hbm = refs[:-8]
    q_ref, k_ref, g_ref, x_ref, right_ref, done_ref, in_sems, out_sems = refs[-8:]
    n_y = len(keyed_hbm)
    width = k_ref.shape[1]
    chunks, _, chunk = x_ref.shape
    moves = start_all(
        [(k_hbm, k_ref), (q_hbm, q_ref), (g_hbm, g_ref)]
        + [(x_hbm.at[:, pl.ds(c * chunk, chunk)], x_ref.at[c]) for c in range(chunks)],
        in_sems,
    )
    y = info_ref[1]
    moves[0].wait()
    for n in range(n_y):
        right_ref[:, lanes(n)] = k_ref[:, lanes(lax.rem(y + n, n_y))]
    moves[1].wait()
    moves[2].wait()
    blocks = q_ref.shape[0] // D
    for h in range(n_y):
        s = lanes(h)
        head = info_ref[0] * n_y + h
        diag = diagonal(head, weight_ref, True)
        for j in range(blocks):
            rows = slice(j * D, (j + 1) * D)
            scores = dot(k_ref[rows, s], q_ref[j * D :, s], 1, 1)
            mixed = weighted(scores, j, j, head, weight_ref, diag)
            res = dot(mixed, g_ref[j * D :, s], 1, 0)
            loc_ref[rows, s] = res
            right_ref[rows, width + h * D : width + (h + 1) * D] = res.astype(bf16)
    sent = []
    for c in range(chunks):
        moves[3 + c].wait()
        part = pl.ds(c * chunk, chunk)
        res = dot(x_ref[c], right_ref[...], 0, 0).astype(bf16)
        for n in range(2 * n_y):
            done_ref[c, n, :, :] = res[:, lanes(n)]
        sent += start_all(
            [(done_ref.at[c, n], keyed_hbm[n].at[part, :]) for n in range(n_y)]
            + [(done_ref.at[c, pl.ds(n_y, n_y)], proj_hbm.at[:, part, :])],
            out_sems.at[c],
        )
    for move in sent:
        move.wait()


def turn_kernel(in_ref, out_ref):
    each = out_ref.shape[2]
    for z in range(out_ref.shape[0]):
        for y in range(out_ref.shape[1]):
            out_ref[z, y, :, :] = in_ref[y, z * each : (z + 1) * each, :]


def tree_kernel(info_ref, weight_ref, in_ref, out_ref):
    nz, ny = in_ref.shape[:2]
    count = nz * ny
    depth = count.bit_length() - 1
    head = info_ref[0] * ny + info_ref[1]
    is_grad = info_ref[2] < nz // 2
    sums = [[in_ref[c % nz, c // nz].astype(f32) for c in range(count)]]
    for bit in range(depth - 1):
        last = sums[-1]
        sums.append([last[2 * b] + last[2 * b + 1] for b in range(len(last) // 2)])
    total = [jnp.zeros(in_ref.shape[2:], f32)]
    for bit in reversed(range(depth)):
        w = lam(D.bit_length() + 2 + bit, head, weight_ref)
        later = jnp.where(is_grad, w, f32(0.0))
        earlier = jnp.where(is_grad, f32(0.0), w)
        last = sums[bit]
        total = [
            total[b // 2] + (later * last[b + 1] if b % 2 == 0 else earlier * last[b - 1])
            for b in range(len(last))
        ]
    for c in range(count):
        out_ref[c % nz, c // nz] = total[c].astype(bf16)


def project_kernel(info_ref, a0, a1, a2, a3, loc_hbm, r_hbm, out_hbm, *refs):
    own_hbm = refs[:-8]
    a_ref, loc_ref, r_ref, done_ref, r_sem, a_sems, out_sems, own_sems = refs[-8:]
    keyed = (a0, a1, a2, a3)
    n_y = len(keyed)
    chunks, rows = loc_ref.shape[:2]
    got = start_all([(r_hbm, r_ref)], r_sem)
    moves = []
    for c in range(chunks):
        part = pl.ds(c * rows, rows)
        moves.append(
            start_all(
                [(keyed[n].at[part, :], a_ref.at[c, n]) for n in range(n_y)]
                + [(loc_hbm.at[part, :], loc_ref.at[c])],
                a_sems.at[c],
            )
        )
    y = info_ref[1]
    half = r_ref.shape[0] // 2
    nz = out_hbm.shape[0]
    each = out_hbm.shape[1] // n_y
    got[0].wait()
    states = [r_ref[:half, lax.rem(y + n_y - n, n_y)].reshape(D, D) for n in range(n_y)]
    states = jnp.concatenate(states, axis=0)
    sent = []
    for c in range(chunks):
        for move in moves[c]:
            move.wait()
        left = jnp.concatenate([a_ref[c, n] for n in range(n_y)], axis=1)
        res = (loc_ref[c].astype(f32) + dot(left, states, 1, 0)).astype(bf16)
        inner = rows // (nz * each)
        for b in range(inner):
            for z in range(nz):
                done_ref[c, z, b * each : (b + 1) * each, :] = res[
                    (b * nz + z) * each : (b * nz + z + 1) * each, :
                ]
        sent += start_all(
            [(done_ref.at[c], out_hbm.at[:, pl.ds(c * inner * each, inner * each), :])],
            out_sems.at[pl.ds(c, 1)],
        )
    sent += start_all(
        [(r_ref.at[:, lax.rem(y + n, n_y)], own_hbm[n]) for n in range(n_y)], own_sems
    )
    for move in sent:
        move.wait()


def outputs_kernel(
    info_ref, weight_ref, q_ref, k_ref, v_ref, g_ref, loc_ref, r0, r1, r2, r3, dq_ref, dk_ref, dv_ref, end_ref
):
    states = (r0, r1, r2, r3)
    n_y = len(states)
    end_ref[...] = jnp.zeros_like(end_ref)
    blocks = q_ref.shape[0] // D
    for n in range(n_y):
        h = lax.rem(info_ref[1] + n_y - n, n_y)
        s = lanes(h)
        head = info_ref[0] * n_y + h
        both = states[n][...].reshape(2 * D, D)
        returned, carried = both[:D], both[D:]
        query, keys, values, grad = q_ref[:, s], k_ref[:, s], v_ref[:, s], g_ref[:, s]
        dv_ref[:, s] = (loc_ref[:, s] + dot(keys, returned, 1, 0)).astype(bf16)
        base_k = dot(values, returned, 1, 1)
        base_q = dot(grad, carried, 1, 1)
        diag = diagonal(head, weight_ref, False)
        diag_t = diagonal(head, weight_ref, True)
        for i in range(blocks):
            rows = slice(i * D, (i + 1) * D)
            upto = (i + 1) * D
            before = dot(grad[rows], values[:upto], 1, 1)
            dmix = weighted(before, 0, i, head, weight_ref, diag)
            dq_ref[rows, s] = (base_q[rows] + dot(dmix, keys[:upto], 1, 0)).astype(bf16)
            later = dot(values[rows], grad[i * D :], 1, 1)
            dmix_t = weighted(later, i, i, head, weight_ref, diag_t)
            dk_ref[rows, s] = (base_k[rows] + dot(dmix_t, query[i * D :], 1, 0)).astype(bf16)


def shard_kernel(in_ref, out_ref, square_ref):
    total = in_ref[0].astype(f32)
    for z in range(1, in_ref.shape[0]):
        total = total + in_ref[z].astype(f32)
    out_ref[...] = total
    square = jnp.sum(jnp.sum(total * total, axis=0, keepdims=True), axis=1, keepdims=True)
    square_ref[...] = jnp.broadcast_to(square[None], square_ref.shape)


def stage_kernel(info_ref, square_ref, shard_ref, out_ref, *part_refs):
    n_y = len(part_refs)
    rows = part_refs[0].shape[0]
    square = jnp.sum(square_ref[...], axis=0, keepdims=True)
    out_ref[...] = jnp.broadcast_to(square, out_ref.shape)
    for n in range(n_y):
        first = pl.multiple_of(lax.rem(info_ref[1] + n, n_y) * rows, rows)
        part_refs[n][...] = shard_ref[pl.ds(first, rows), :]


def final_kernel(info_ref, mom_ref, p0, p1, p2, p3, total_ref, out_ref):
    parts = (p0, p1, p2, p3)
    n_y = len(parts)
    total = jnp.sum(total_ref[...], axis=0)
    factor = jnp.minimum(f32(1.0), clip_norm / jnp.sqrt(total + 1e-06))
    for n in range(n_y):
        s = lanes(lax.rem(info_ref[1] + n_y - n, n_y))
        out_ref[:, s] = momentum_rate * mom_ref[:, s] + factor * parts[n][...]


def shift(x, axis, by):
    n = lax.axis_size(axis)
    return lax.ppermute(x, axis, [(i, (i + by) % n) for i in range(n)])


def swap(x, axes):
    return lax.all_to_all(x, axes, 0, 0, tiled=True)


def body(queries, keys, values, out_grad, inputs, momentum, level_weight):
    length, width = queries.shape
    features = inputs.shape[1]
    n_y, n_z = lax.axis_size(Y), lax.axis_size(Z)
    heads = width // D
    sds = jax.ShapeDtypeStruct
    info = jnp.stack(
        [lax.axis_index(HEAD), lax.axis_index(Y), lax.axis_index(Z), jnp.int32(0)]
    ).astype(jnp.int32)

    square_sds = sds((length, width), bf16)
    held = pltpu.VMEM((length, width), bf16)
    dma = pltpu.SemaphoreType.DMA
    both = call(
        states_kernel,
        sds((heads, 2 * D, D), bf16),
        (queries, out_grad, keys, values),
        4 * length * width * D,
        [ANY] * 4,
        scratch=[held] * 4 + [dma((4,))],
        vmem=VMEM_ALL,
    )
    chunk = 512
    chunks = features // chunk
    local, proj, *keyed = call(
        local_kernel,
        (sds((length, width), f32), sds((heads, features, D), bf16))
        + tuple(sds((features, D), bf16) for _ in range(n_y)),
        (queries, keys, out_grad, inputs),
        4 * length * width * features + 3 * length * length * width,
        [ANY] * 4,
        (VMEM,) + (ANY,) * (n_y + 1),
        scratch=[held] * 3
        + [
            pltpu.VMEM((chunks, length, chunk), bf16),
            pltpu.VMEM((length, 2 * width), bf16),
            pltpu.VMEM((chunks, 2 * n_y, chunk, D), bf16),
            dma((3 + chunks,)),
            dma((chunks, n_y + 1)),
        ],
        scalars=(info, level_weight),
        vmem=VMEM_ALL,
    )
    both, proj, *keyed[1:] = call(
        turn_kernel,
        sds((n_z, n_y, 2 * D // n_z, D), bf16),
        (swap(both, Y),),
        1 << 16,
        gated=(proj, *keyed[1:]),
        vmem=VMEM_ALL,
    )
    both = swap(both, Z)
    keyed = [keyed[0]] + [shift(keyed[n], Y, n) for n in range(1, n_y)]
    proj = lax.psum_scatter(
        proj.reshape(heads * features, D), Y, scatter_dimension=0, tiled=True
    )

    both = call(
        tree_kernel,
        sds(both.shape, bf16),
        (both,),
        1 << 21,
        scalars=(info, level_weight),
        after=(keyed[1],),
        vmem=8,
    )
    both = swap(both, Z)

    rows = features // 2
    parts, *own = call(
        project_kernel,
        (sds((n_z, features // n_z, D), bf16),)
        + tuple(sds((n_z, 2 * D // n_z, D), bf16) for _ in range(n_y)),
        (*keyed, proj, both),
        2 * features * n_y * D * D,
        [ANY] * (n_y + 2),
        (ANY,) * (n_y + 1),
        scratch=[
            pltpu.VMEM((2, n_y, rows, D), bf16),
            pltpu.VMEM((2, rows, D), bf16),
            pltpu.VMEM(both.shape, bf16),
            pltpu.VMEM((2, n_z, rows // n_z, D), bf16),
            dma((1,)),
            dma((2, n_y + 1)),
            dma((2,)),
            dma((n_y,)),
        ],
        scalars=(info,),
        vmem=VMEM_ALL,
    )
    parts = swap(parts, Z)

    own = [own[0]] + [shift(own[n], Y, n) for n in range(1, n_y)]
    query_grad, key_grad, value_grad, end = call(
        outputs_kernel,
        (sds((length, width), bf16),) * 3 + (sds((8, D), f32),),
        (queries, keys, values, out_grad, local, *own),
        6 * length * length * width,
        scalars=(info, level_weight),
        vmem=VMEM_ALL,
    )

    near, rest = HEAD + (Y,), (Z,)
    rows = momentum.shape[0]
    shard, square = call(
        shard_kernel,
        (sds((n_y * rows, D), f32), sds((lax.axis_size(near), 1, D), f32)),
        (parts,),
        1 << 20,
        after=(end,),
        vmem=8,
    )
    square = swap(square, near)
    total, *mine = call(
        stage_kernel,
        (sds((lax.axis_size(rest), 1, D), f32),) + tuple(sds((rows, D), f32) for _ in range(n_y)),
        (square, shard),
        1 << 16,
        scalars=(info,),
        vmem=8,
    )
    total = swap(total, rest)
    mine = [mine[0]] + [shift(mine[n], Y, n) for n in range(1, n_y)]
    new_momentum = call(
        final_kernel,
        sds(momentum.shape, f32),
        (momentum, *mine, total),
        1 << 16,
        scalars=(info,),
        vmem=8,
    )
    return (query_grad, key_grad, value_grad, new_momentum)


def solution(mesh):
    torus = Mesh(mesh.devices.reshape(4, 2, 4, 16), HEAD + SEQ)
    tokens = P(SEQ, HEAD)
    return jax.shard_map(
        body,
        mesh=torus,
        in_specs=(tokens, tokens, tokens, tokens, P(SEQ, None), tokens, P()),
        out_specs=(tokens, tokens, tokens, tokens),
        check_vma=False,
    )
```

```python
import functools
import math

import jax
import jax.numpy as jnp
import numpy as np
from jax import lax
from jax.experimental import pallas as pl
from jax.experimental.pallas import tpu as pltpu
from jax.sharding import Mesh
from jax.sharding import PartitionSpec as P

D = 128
HEAD = ("head_0", "head_1")
Y = "seq_0"
Z = "seq_1"
SEQ = (Y, Z)

VMEM_ALL = 60

clip_norm = 1024.0
momentum_rate = 0.9

bf16 = jnp.bfloat16
f32 = jnp.float32


def dot(a, b, ca, cb):
    return lax.dot_general(a, b, (((ca,), (cb,)), ((), ())), preferred_element_type=f32)


VMEM = pl.BlockSpec(memory_space=pltpu.VMEM)
ANY = pl.BlockSpec(memory_space=pl.ANY)


def call(kernel, out_shape, operands, flops, in_specs=None, out_specs=None, grid=(), scratch=(), vmem=16, after=(), scalars=(), gated=()):
    leaves = jax.tree.leaves((operands, out_shape))
    n = len(scalars) + len(operands)
    skip = n + len(after) + len(gated)
    last = skip + len(jax.tree.leaves(out_shape))

    def run(*refs):
        kernel(*refs[:n], *refs[skip:last], *refs[last + len(gated) :])

    in_specs = list(in_specs or [None] * len(operands))
    in_specs = [VMEM if i is None else i for i in in_specs]
    if out_specs is None:
        out_specs = jax.tree.map(lambda _: VMEM, out_shape)
    anywhere = ANY
    aliases = {}
    if gated:
        first = len(jax.tree.leaves(out_shape))
        aliases = {n + len(after) + i: first + i for i in range(len(gated))}
        out_shape = (*jax.tree.leaves(out_shape), *(jax.ShapeDtypeStruct(x.shape, x.dtype) for x in gated))
        out_specs = (*jax.tree.leaves(out_specs), *(anywhere for _ in gated))
    return pl.pallas_call(
        run,
        out_shape=out_shape,
        grid_spec=pltpu.PrefetchScalarGridSpec(
            num_scalar_prefetch=len(scalars),
            grid=grid,
            in_specs=in_specs + [anywhere] * (len(after) + len(gated)),
            out_specs=out_specs,
            scratch_shapes=list(scratch),
        ),
        input_output_aliases=aliases,
        compiler_params=pltpu.CompilerParams(vmem_limit_bytes=vmem * 1024 * 1024),
        cost_estimate=pl.CostEstimate(
            flops=flops,
            bytes_accessed=sum(x.size * x.dtype.itemsize for x in leaves),
            transcendentals=0,
        ),
    )(*scalars, *operands, *after, *gated)


def lanes(block):
    if isinstance(block, int):
        return slice(block * D, (block + 1) * D)
    return pl.ds(pl.multiple_of(block * D, D), D)


def lam(level, head, weight_ref):
    factor = np.float32(2.0 ** (-0.5 * level) / (8.0 * math.sqrt(D)))
    return weight_ref[level, head].astype(f32) * factor


def diagonal(head, weight_ref, transposed):
    row = lax.broadcasted_iota(jnp.int32, (D, D), 0)
    col = lax.broadcasted_iota(jnp.int32, (D, D), 1)
    apart = jnp.bitwise_xor(row, col)
    out = jnp.full((D, D), lam(0, head, weight_ref), f32)
    for level in range(1, D.bit_length()):
        out = jnp.where(apart >= 1 << (level - 1), lam(level, head, weight_ref), out)
    keep = row <= col if transposed else col <= row
    return jnp.where(keep, out, f32(0.0))


def far(i, j, head, weight_ref):
    return lam(D.bit_length() - 1 + (i ^ j).bit_length(), head, weight_ref)


def weighted(scores, first, own, head, weight_ref, diag):
    count = scores.shape[1] // D
    parts = []
    for n in range(count):
        part = scores[:, n * D : (n + 1) * D]
        w = diag if first + n == own else far(first + n, own, head, weight_ref)
        parts.append((w * part).astype(bf16))
    return parts[0] if count == 1 else jnp.concatenate(parts, axis=1)


def start_all(pairs, sems):
    moves = [pltpu.make_async_copy(source, to, sems.at[i]) for i, (source, to) in enumerate(pairs)]
    for move in moves:
        move.start()
    return moves


def states_kernel(q_hbm, g_hbm, k_hbm, v_hbm, out_ref, q_ref, g_ref, k_ref, v_ref, sems):
    moves = start_all(
        [(q_hbm, q_ref), (g_hbm, g_ref), (k_hbm, k_ref), (v_hbm, v_ref)], sems
    )
    moves[0].wait()
    moves[1].wait()
    for h in range(out_ref.shape[0]):
        s = lanes(h)
        out_ref[h, :D, :] = dot(q_ref[:, s], g_ref[:, s], 0, 0).astype(bf16)
    moves[2].wait()
    moves[3].wait()
    for h in range(out_ref.shape[0]):
        s = lanes(h)
        out_ref[h, D:, :] = dot(k_ref[:, s], v_ref[:, s], 0, 0).astype(bf16)


def local_kernel(info_ref, weight_ref, q_hbm, k_hbm, g_hbm, x_hbm, loc_ref, proj_hbm, *refs):
    keyed_hbm = refs[:-9]
    q_ref, k_ref, g_ref, x_ref, right_ref, done_ref, summed_ref, in_sems, out_sems = refs[-9:]
    n_y = len(keyed_hbm)
    nz, each = summed_ref.shape[1], summed_ref.shape[3]
    width = k_ref.shape[1]
    chunks, _, chunk = x_ref.shape
    moves = start_all(
        [(k_hbm, k_ref), (q_hbm, q_ref), (g_hbm, g_ref)]
        + [(x_hbm.at[:, pl.ds(c * chunk, chunk)], x_ref.at[c]) for c in range(chunks)],
        in_sems,
    )
    y = info_ref[1]
    moves[0].wait()
    for n in range(n_y):
        right_ref[:, lanes(n)] = k_ref[:, lanes(lax.rem(y + n, n_y))]
    moves[1].wait()
    moves[2].wait()
    blocks = q_ref.shape[0] // D
    for h in range(n_y):
        s = lanes(h)
        head = info_ref[0] * n_y + h
        diag = diagonal(head, weight_ref, True)
        for j in range(blocks):
            rows = slice(j * D, (j + 1) * D)
            scores = dot(k_ref[rows, s], q_ref[j * D :, s], 1, 1)
            mixed = weighted(scores, j, j, head, weight_ref, diag)
            res = dot(mixed, g_ref[j * D :, s], 1, 0)
            loc_ref[rows, s] = res
            right_ref[rows, width + h * D : width + (h + 1) * D] = res.astype(bf16)
    sent = []
    for c in range(chunks):
        moves[3 + c].wait()
        part = pl.ds(c * chunk, chunk)
        res = dot(x_ref[c], right_ref[...], 0, 0).astype(bf16)
        for n in range(n_y):
            done_ref[c, n, :, :] = res[:, lanes(n)]
            for z in range(nz):
                summed_ref[c, z, n, :, :] = res[z * each : (z + 1) * each, lanes(n_y + n)]
        sent += start_all(
            [(done_ref.at[c, n], keyed_hbm[n].at[part, :]) for n in range(n_y)]
            + [(summed_ref.at[c], proj_hbm.at[:, :, pl.ds(c * each, each), :])],
            out_sems.at[c],
        )
    for move in sent:
        move.wait()


def turn_kernel(in_ref, out_ref):
    each = out_ref.shape[2]
    for z in range(out_ref.shape[0]):
        for y in range(out_ref.shape[1]):
            out_ref[z, y, :, :] = in_ref[y, z * each : (z + 1) * each, :]


def tree_kernel(info_ref, weight_ref, in_ref, out_ref):
    nz, ny = in_ref.shape[:2]
    count = nz * ny
    depth = count.bit_length() - 1
    head = info_ref[0] * ny + info_ref[1]
    is_grad = info_ref[2] < nz // 2
    sums = [[in_ref[c % nz, c // nz].astype(f32) for c in range(count)]]
    for bit in range(depth - 1):
        last = sums[-1]
        sums.append([last[2 * b] + last[2 * b + 1] for b in range(len(last) // 2)])
    total = [jnp.zeros(in_ref.shape[2:], f32)]
    for bit in reversed(range(depth)):
        w = lam(D.bit_length() + 2 + bit, head, weight_ref)
        later = jnp.where(is_grad, w, f32(0.0))
        earlier = jnp.where(is_grad, f32(0.0), w)
        last = sums[bit]
        total = [
            total[b // 2] + (later * last[b + 1] if b % 2 == 0 else earlier * last[b - 1])
            for b in range(len(last))
        ]
    for c in range(count):
        out_ref[c % nz, c // nz] = total[c].astype(bf16)


def project_kernel(info_ref, a0, a1, a2, a3, r_hbm, out_hbm, *refs):
    own_hbm = refs[:-7]
    a_ref, r_ref, done_ref, r_sem, a_sems, out_sems, own_sems = refs[-7:]
    keyed = (a0, a1, a2, a3)
    n_y = len(keyed)
    chunks, _, rows = a_ref.shape[:3]
    got = start_all([(r_hbm, r_ref)], r_sem)
    moves = []
    for c in range(chunks):
        part = pl.ds(c * rows, rows)
        moves.append(
            start_all(
                [(keyed[n].at[part, :], a_ref.at[c, n]) for n in range(n_y)], a_sems.at[c]
            )
        )
    y = info_ref[1]
    half = r_ref.shape[0] // 2
    nz = out_hbm.shape[0]
    each = out_hbm.shape[1] // n_y
    got[0].wait()
    states = [r_ref[:half, lax.rem(y + n_y - n, n_y)].reshape(D, D) for n in range(n_y)]
    states = jnp.concatenate(states, axis=0)
    sent = []
    for c in range(chunks):
        for move in moves[c]:
            move.wait()
        left = jnp.concatenate([a_ref[c, n] for n in range(n_y)], axis=1)
        res = dot(left, states, 1, 0).astype(bf16)
        inner = rows // (nz * each)
        for b in range(inner):
            for z in range(nz):
                done_ref[c, z, b * each : (b + 1) * each, :] = res[
                    (b * nz + z) * each : (b * nz + z + 1) * each, :
                ]
        sent += start_all(
            [(done_ref.at[c], out_hbm.at[:, pl.ds(c * inner * each, inner * each), :])],
            out_sems.at[pl.ds(c, 1)],
        )
    sent += start_all(
        [(r_ref.at[:, lax.rem(y + n, n_y)], own_hbm[n]) for n in range(n_y)], own_sems
    )
    for move in sent:
        move.wait()


def outputs_kernel(
    info_ref, weight_ref, q_ref, k_ref, v_ref, g_ref, loc_ref, r0, r1, r2, r3, dq_ref, dk_ref, dv_ref, end_ref
):
    states = (r0, r1, r2, r3)
    n_y = len(states)
    end_ref[...] = jnp.zeros_like(end_ref)
    blocks = q_ref.shape[0] // D
    for n in range(n_y):
        h = lax.rem(info_ref[1] + n_y - n, n_y)
        s = lanes(h)
        head = info_ref[0] * n_y + h
        both = states[n][...].reshape(2 * D, D)
        returned, carried = both[:D], both[D:]
        query, keys, values, grad = q_ref[:, s], k_ref[:, s], v_ref[:, s], g_ref[:, s]
        dv_ref[:, s] = (loc_ref[:, s] + dot(keys, returned, 1, 0)).astype(bf16)
        base_k = dot(values, returned, 1, 1)
        base_q = dot(grad, carried, 1, 1)
        diag = diagonal(head, weight_ref, False)
        diag_t = diagonal(head, weight_ref, True)
        for i in range(blocks):
            rows = slice(i * D, (i + 1) * D)
            upto = (i + 1) * D
            before = dot(grad[rows], values[:upto], 1, 1)
            dmix = weighted(before, 0, i, head, weight_ref, diag)
            dq_ref[rows, s] = (base_q[rows] + dot(dmix, keys[:upto], 1, 0)).astype(bf16)
            later = dot(values[rows], grad[i * D :], 1, 1)
            dmix_t = weighted(later, i, i, head, weight_ref, diag_t)
            dk_ref[rows, s] = (base_k[rows] + dot(dmix_t, query[i * D :], 1, 0)).astype(bf16)


def shard_kernel(info_ref, in_ref, loc_ref, square_ref, *refs):
    part_refs, total_ref = refs[:-1], refs[-1]
    n_y = len(part_refs)
    rows = part_refs[0].shape[0]
    total = loc_ref[...].astype(f32)
    for z in range(in_ref.shape[0]):
        total = total + in_ref[z].astype(f32)
    total_ref[...] = total
    square = jnp.sum(jnp.sum(total * total, axis=0, keepdims=True), axis=1, keepdims=True)
    square_ref[...] = jnp.broadcast_to(square[None], square_ref.shape)
    for n in range(n_y):
        first = pl.multiple_of(lax.rem(info_ref[1] + n, n_y) * rows, rows)
        part_refs[n][...] = total_ref[pl.ds(first, rows), :]


def stage_kernel(square_ref, out_ref):
    square = jnp.sum(square_ref[...], axis=0, keepdims=True)
    out_ref[...] = jnp.broadcast_to(square, out_ref.shape)


def final_kernel(info_ref, mom_ref, p0, p1, p2, p3, total_ref, out_ref):
    parts = (p0, p1, p2, p3)
    n_y = len(parts)
    total = jnp.sum(total_ref[...], axis=0)
    factor = jnp.minimum(f32(1.0), clip_norm / jnp.sqrt(total + 1e-06))
    for n in range(n_y):
        s = lanes(lax.rem(info_ref[1] + n_y - n, n_y))
        out_ref[:, s] = momentum_rate * mom_ref[:, s] + factor * parts[n][...]


def shift(x, axis, by):
    n = lax.axis_size(axis)
    return lax.ppermute(x, axis, [(i, (i + by) % n) for i in range(n)])


def swap(x, axes):
    return lax.all_to_all(x, axes, 0, 0, tiled=True)


def body(queries, keys, values, out_grad, inputs, momentum, level_weight):
    length, width = queries.shape
    features = inputs.shape[1]
    n_y, n_z = lax.axis_size(Y), lax.axis_size(Z)
    heads = width // D
    sds = jax.ShapeDtypeStruct
    info = jnp.stack(
        [lax.axis_index(HEAD), lax.axis_index(Y), lax.axis_index(Z), jnp.int32(0)]
    ).astype(jnp.int32)

    square_sds = sds((length, width), bf16)
    held = pltpu.VMEM((length, width), bf16)
    dma = pltpu.SemaphoreType.DMA
    both = call(
        states_kernel,
        sds((heads, 2 * D, D), bf16),
        (queries, out_grad, keys, values),
        4 * length * width * D,
        [ANY] * 4,
        scratch=[held] * 4 + [dma((4,))],
        vmem=VMEM_ALL,
    )
    chunk = 512
    chunks = features // chunk
    local, proj, *keyed = call(
        local_kernel,
        (sds((length, width), f32), sds((n_z, heads, features // n_z, D), bf16))
        + tuple(sds((features, D), bf16) for _ in range(n_y)),
        (queries, keys, out_grad, inputs),
        4 * length * width * features + 3 * length * length * width,
        [ANY] * 4,
        (VMEM,) + (ANY,) * (n_y + 1),
        scratch=[held] * 3
        + [
            pltpu.VMEM((chunks, length, chunk), bf16),
            pltpu.VMEM((length, 2 * width), bf16),
            pltpu.VMEM((chunks, n_y, chunk, D), bf16),
            pltpu.VMEM((chunks, n_z, heads, chunk // n_z, D), bf16),
            dma((3 + chunks,)),
            dma((chunks, n_y + 1)),
        ],
        scalars=(info, level_weight),
        vmem=VMEM_ALL,
    )
    both, proj, *keyed[1:] = call(
        turn_kernel,
        sds((n_z, n_y, 2 * D // n_z, D), bf16),
        (swap(both, Y),),
        1 << 16,
        gated=(proj, *keyed[1:]),
        vmem=VMEM_ALL,
    )
    both = swap(both, Z)
    keyed = [keyed[0]] + [shift(keyed[n], Y, n) for n in range(1, n_y)]
    proj = proj.reshape(heads * features, D)
    for axis in (Z, Y):
        proj = lax.psum_scatter(proj, axis, scatter_dimension=0, tiled=True)

    both = call(
        tree_kernel,
        sds(both.shape, bf16),
        (both,),
        1 << 21,
        scalars=(info, level_weight),
        after=(keyed[1], keyed[3]),
        vmem=8,
    )
    both = swap(both, Z)

    rows = features // 2
    parts, *own = call(
        project_kernel,
        (sds((n_z, features // n_z, D), bf16),)
        + tuple(sds((n_z, 2 * D // n_z, D), bf16) for _ in range(n_y)),
        (*keyed, both),
        2 * features * n_y * D * D,
        [ANY] * (n_y + 1),
        (ANY,) * (n_y + 1),
        scratch=[
            pltpu.VMEM((2, n_y, rows, D), bf16),
            pltpu.VMEM(both.shape, bf16),
            pltpu.VMEM((2, n_z, rows // n_z, D), bf16),
            dma((1,)),
            dma((2, n_y)),
            dma((2,)),
            dma((n_y,)),
        ],
        scalars=(info,),
        vmem=VMEM_ALL,
    )
    parts = swap(parts, Z)

    own = [own[0]] + [shift(own[n], Y, n) for n in range(1, n_y)]
    query_grad, key_grad, value_grad, end = call(
        outputs_kernel,
        (sds((length, width), bf16),) * 3 + (sds((8, D), f32),),
        (queries, keys, values, out_grad, local, *own),
        6 * length * length * width,
        scalars=(info, level_weight),
        vmem=VMEM_ALL,
    )

    near, rest = HEAD + (Y,), (Z,)
    rows = momentum.shape[0]
    square, *mine = call(
        shard_kernel,
        (sds((lax.axis_size(near), 1, D), f32),) + (sds((rows, D), f32),) * n_y,
        (parts, proj),
        1 << 20,
        scratch=[pltpu.VMEM((n_y * rows, D), f32)],
        scalars=(info,),
        after=(end,),
        vmem=8,
    )
    mine = [mine[0]] + [shift(mine[n], Y, n) for n in range(1, n_y)]
    square = swap(square, near)
    total = call(
        stage_kernel,
        sds((lax.axis_size(rest), 1, D), f32),
        (square,),
        1 << 16,
        after=(mine[1],),
        vmem=8,
    )
    total = swap(total, rest)
    new_momentum = call(
        final_kernel,
        sds(momentum.shape, f32),
        (momentum, *mine, total),
        1 << 16,
        scalars=(info,),
        vmem=8,
    )
    return (query_grad, key_grad, value_grad, new_momentum)


def solution(mesh):
    torus = Mesh(mesh.devices.reshape(4, 2, 4, 16), HEAD + SEQ)
    tokens = P(SEQ, HEAD)
    return jax.shard_map(
        body,
        mesh=torus,
        in_specs=(tokens, tokens, tokens, tokens, P(SEQ, None), tokens, P()),
        out_specs=(tokens, tokens, tokens, tokens),
        check_vma=False,
    )
```

```python
import functools
import math

import jax
import jax.numpy as jnp
import numpy as np
from jax import lax
from jax.experimental import pallas as pl
from jax.experimental.pallas import tpu as pltpu
from jax.sharding import Mesh
from jax.sharding import PartitionSpec as P

D = 128
HEAD = ("head_0", "head_1")
Y = "seq_0"
Z = "seq_1"
SEQ = (Y, Z)

VMEM_ALL = 60

clip_norm = 1024.0
momentum_rate = 0.9

bf16 = jnp.bfloat16
f32 = jnp.float32


def dot(a, b, ca, cb):
    return lax.dot_general(a, b, (((ca,), (cb,)), ((), ())), preferred_element_type=f32)


VMEM = pl.BlockSpec(memory_space=pltpu.VMEM)
ANY = pl.BlockSpec(memory_space=pl.ANY)


def call(kernel, out_shape, operands, flops, in_specs=None, out_specs=None, grid=(), scratch=(), vmem=16, after=(), scalars=(), gated=()):
    leaves = jax.tree.leaves((operands, out_shape))
    n = len(scalars) + len(operands)
    skip = n + len(after) + len(gated)
    last = skip + len(jax.tree.leaves(out_shape))

    def run(*refs):
        kernel(*refs[:n], *refs[skip:last], *refs[last + len(gated) :])

    in_specs = list(in_specs or [None] * len(operands))
    in_specs = [VMEM if i is None else i for i in in_specs]
    if out_specs is None:
        out_specs = jax.tree.map(lambda _: VMEM, out_shape)
    anywhere = ANY
    aliases = {}
    if gated:
        first = len(jax.tree.leaves(out_shape))
        aliases = {n + len(after) + i: first + i for i in range(len(gated))}
        out_shape = (*jax.tree.leaves(out_shape), *(jax.ShapeDtypeStruct(x.shape, x.dtype) for x in gated))
        out_specs = (*jax.tree.leaves(out_specs), *(anywhere for _ in gated))
    return pl.pallas_call(
        run,
        out_shape=out_shape,
        grid_spec=pltpu.PrefetchScalarGridSpec(
            num_scalar_prefetch=len(scalars),
            grid=grid,
            in_specs=in_specs + [anywhere] * (len(after) + len(gated)),
            out_specs=out_specs,
            scratch_shapes=list(scratch),
        ),
        input_output_aliases=aliases,
        compiler_params=pltpu.CompilerParams(vmem_limit_bytes=vmem * 1024 * 1024),
        cost_estimate=pl.CostEstimate(
            flops=flops,
            bytes_accessed=sum(x.size * x.dtype.itemsize for x in leaves),
            transcendentals=0,
        ),
    )(*scalars, *operands, *after, *gated)


def lanes(block):
    if isinstance(block, int):
        return slice(block * D, (block + 1) * D)
    return pl.ds(pl.multiple_of(block * D, D), D)


def lam(level, head, weight_ref):
    factor = np.float32(2.0 ** (-0.5 * level) / (8.0 * math.sqrt(D)))
    return weight_ref[level, head].astype(f32) * factor


def diagonal(head, weight_ref, transposed):
    row = lax.broadcasted_iota(jnp.int32, (D, D), 0)
    col = lax.broadcasted_iota(jnp.int32, (D, D), 1)
    apart = jnp.bitwise_xor(row, col)
    out = jnp.full((D, D), lam(0, head, weight_ref), f32)
    for level in range(1, D.bit_length()):
        out = jnp.where(apart >= 1 << (level - 1), lam(level, head, weight_ref), out)
    keep = row <= col if transposed else col <= row
    return jnp.where(keep, out, f32(0.0))


def far(i, j, head, weight_ref):
    return lam(D.bit_length() - 1 + (i ^ j).bit_length(), head, weight_ref)


def weighted(scores, first, own, head, weight_ref, diag):
    count = scores.shape[1] // D
    parts = []
    for n in range(count):
        part = scores[:, n * D : (n + 1) * D]
        w = diag if first + n == own else far(first + n, own, head, weight_ref)
        parts.append((w * part).astype(bf16))
    return parts[0] if count == 1 else jnp.concatenate(parts, axis=1)


def start_all(pairs, sems):
    moves = [pltpu.make_async_copy(source, to, sems.at[i]) for i, (source, to) in enumerate(pairs)]
    for move in moves:
        move.start()
    return moves


def states_kernel(q_hbm, g_hbm, k_hbm, v_hbm, out_ref, q_ref, g_ref, k_ref, v_ref, sems):
    moves = start_all(
        [(q_hbm, q_ref), (g_hbm, g_ref), (k_hbm, k_ref), (v_hbm, v_ref)], sems
    )
    moves[0].wait()
    moves[1].wait()
    for h in range(out_ref.shape[0]):
        s = lanes(h)
        out_ref[h, :D, :] = dot(q_ref[:, s], g_ref[:, s], 0, 0).astype(bf16)
    moves[2].wait()
    moves[3].wait()
    for h in range(out_ref.shape[0]):
        s = lanes(h)
        out_ref[h, D:, :] = dot(k_ref[:, s], v_ref[:, s], 0, 0).astype(bf16)


def local_kernel(info_ref, weight_ref, q_hbm, k_hbm, g_hbm, x_hbm, loc_ref, *refs):
    out_hbm = refs[:-8]
    q_ref, k_ref, g_ref, x_ref, right_ref, done_ref, in_sems, out_sems = refs[-8:]
    n_y = len(out_hbm)
    chunks, _, chunk = x_ref.shape
    moves = start_all(
        [(k_hbm, k_ref), (q_hbm, q_ref), (g_hbm, g_ref)]
        + [(x_hbm.at[:, pl.ds(c * chunk, chunk)], x_ref.at[c]) for c in range(chunks)],
        in_sems,
    )
    for move in moves[:3]:
        move.wait()
    blocks = q_ref.shape[0] // D
    for n in range(n_y):
        h = lax.rem(info_ref[1] + n, n_y)
        s = lanes(h)
        head = info_ref[0] * n_y + h
        keys, query, grad = k_ref[:, s], q_ref[:, s], g_ref[:, s]
        right_ref[:, lanes(2 * n)] = keys
        diag = diagonal(head, weight_ref, True)
        for j in range(blocks):
            rows = slice(j * D, (j + 1) * D)
            scores = dot(keys[rows], query[j * D :], 1, 1)
            mixed = weighted(scores, j, j, head, weight_ref, diag)
            res = dot(mixed, grad[j * D :], 1, 0)
            loc_ref[rows, s] = res
            right_ref[rows, lanes(2 * n + 1)] = res.astype(bf16)
    sent = []
    for c in range(chunks):
        moves[3 + c].wait()
        res = dot(x_ref[c], right_ref[...], 0, 0).astype(bf16)
        for n in range(n_y):
            done_ref[c, n, 0, :, :] = res[:, lanes(2 * n)]
            done_ref[c, n, 1, :, :] = res[:, lanes(2 * n + 1)]
        part = pl.ds(c * chunk, chunk)
        sent += start_all(
            [(done_ref.at[c, n], out_hbm[n].at[:, part, :]) for n in range(n_y)], out_sems.at[c]
        )
    for move in sent:
        move.wait()


def turn_kernel(in_ref, out_ref):
    each = out_ref.shape[2]
    for z in range(out_ref.shape[0]):
        for y in range(out_ref.shape[1]):
            out_ref[z, y, :, :] = in_ref[y, z * each : (z + 1) * each, :]


def tree_kernel(info_ref, weight_ref, in_ref, out_ref):
    nz, ny = in_ref.shape[:2]
    count = nz * ny
    depth = count.bit_length() - 1
    head = info_ref[0] * ny + info_ref[1]
    is_grad = info_ref[2] < nz // 2
    sums = [[in_ref[c % nz, c // nz].astype(f32) for c in range(count)]]
    for bit in range(depth - 1):
        last = sums[-1]
        sums.append([last[2 * b] + last[2 * b + 1] for b in range(len(last) // 2)])
    total = [jnp.zeros(in_ref.shape[2:], f32)]
    for bit in reversed(range(depth)):
        w = lam(D.bit_length() + 2 + bit, head, weight_ref)
        later = jnp.where(is_grad, w, f32(0.0))
        earlier = jnp.where(is_grad, f32(0.0), w)
        last = sums[bit]
        total = [
            total[b // 2] + (later * last[b + 1] if b % 2 == 0 else earlier * last[b - 1])
            for b in range(len(last))
        ]
    for c in range(count):
        out_ref[c % nz, c // nz] = total[c].astype(bf16)


def project_kernel(info_ref, a0, a1, a2, a3, r_hbm, out_hbm, *refs):
    own_hbm = refs[:-7]
    a_ref, r_ref, done_ref, r_sem, a_sems, out_sems, own_sems = refs[-7:]
    keyed = (a0, a1, a2, a3)
    n_y = len(keyed)
    chunks, _, _, rows, _ = a_ref.shape
    got = start_all([(r_hbm, r_ref)], r_sem)
    moves = []
    for c in range(chunks):
        part = pl.ds(c * rows, rows)
        moves.append(
            start_all(
                [(keyed[n].at[:, part, :], a_ref.at[c, n]) for n in range(n_y)], a_sems.at[c]
            )
        )
    y = info_ref[1]
    half = r_ref.shape[0] // 2
    nz = out_hbm.shape[0]
    each = out_hbm.shape[1] // n_y
    got[0].wait()
    states = [r_ref[:half, lax.rem(y + n_y - n, n_y)].reshape(D, D) for n in range(n_y)]
    states = jnp.concatenate(states, axis=0)
    sent = []
    for c in range(chunks):
        for move in moves[c]:
            move.wait()
        left = jnp.concatenate([a_ref[c, n, 0] for n in range(n_y)], axis=1)
        res = dot(left, states, 1, 0)
        for n in range(n_y):
            res = res + a_ref[c, n, 1].astype(f32)
        res = res.astype(bf16)
        inner = rows // (nz * each)
        for b in range(inner):
            for z in range(nz):
                done_ref[c, z, b * each : (b + 1) * each, :] = res[
                    (b * nz + z) * each : (b * nz + z + 1) * each, :
                ]
        sent += start_all(
            [(done_ref.at[c], out_hbm.at[:, pl.ds(c * inner * each, inner * each), :])],
            out_sems.at[pl.ds(c, 1)],
        )
    sent += start_all(
        [(r_ref.at[:, lax.rem(y + n, n_y)], own_hbm[n]) for n in range(n_y)], own_sems
    )
    for move in sent:
        move.wait()


def outputs_kernel(
    info_ref, weight_ref, q_ref, k_ref, v_ref, g_ref, loc_ref, r0, r1, r2, r3, dq_ref, dk_ref, dv_ref, end_ref
):
    states = (r0, r1, r2, r3)
    n_y = len(states)
    end_ref[...] = jnp.zeros_like(end_ref)
    blocks = q_ref.shape[0] // D
    for n in range(n_y):
        h = lax.rem(info_ref[1] + n_y - n, n_y)
        s = lanes(h)
        head = info_ref[0] * n_y + h
        both = states[n][...].reshape(2 * D, D)
        returned, carried = both[:D], both[D:]
        query, keys, values, grad = q_ref[:, s], k_ref[:, s], v_ref[:, s], g_ref[:, s]
        dv_ref[:, s] = (loc_ref[:, s] + dot(keys, returned, 1, 0)).astype(bf16)
        base_k = dot(values, returned, 1, 1)
        base_q = dot(grad, carried, 1, 1)
        diag = diagonal(head, weight_ref, False)
        diag_t = diagonal(head, weight_ref, True)
        for i in range(blocks):
            rows = slice(i * D, (i + 1) * D)
            upto = (i + 1) * D
            before = dot(grad[rows], values[:upto], 1, 1)
            dmix = weighted(before, 0, i, head, weight_ref, diag)
            dq_ref[rows, s] = (base_q[rows] + dot(dmix, keys[:upto], 1, 0)).astype(bf16)
            later = dot(values[rows], grad[i * D :], 1, 1)
            dmix_t = weighted(later, i, i, head, weight_ref, diag_t)
            dk_ref[rows, s] = (base_k[rows] + dot(dmix_t, query[i * D :], 1, 0)).astype(bf16)


def shard_kernel(info_ref, in_ref, square_ref, out_ref, total_ref):
    n_y, heads, rows = out_ref.shape[:3]
    total = in_ref[0].astype(f32)
    for z in range(1, in_ref.shape[0]):
        total = total + in_ref[z].astype(f32)
    total_ref[...] = total
    square = jnp.sum(jnp.sum(total * total, axis=0, keepdims=True), axis=1, keepdims=True)
    square_ref[...] = jnp.broadcast_to(square[None], square_ref.shape)
    out_ref[...] = jnp.zeros_like(out_ref)
    for y in range(n_y):
        out_ref[y, info_ref[1], :, :] = total_ref[y * rows : (y + 1) * rows, :]


def stage_kernel(square_ref, out_ref):
    square = jnp.sum(square_ref[...], axis=0, keepdims=True)
    out_ref[...] = jnp.broadcast_to(square, out_ref.shape)


def final_kernel(mom_ref, in_ref, total_ref, out_ref):
    total = jnp.sum(total_ref[...], axis=0)
    factor = jnp.minimum(f32(1.0), clip_norm / jnp.sqrt(total + 1e-06))
    for h in range(in_ref.shape[0]):
        s = lanes(h)
        out_ref[:, s] = momentum_rate * mom_ref[:, s] + factor * in_ref[h]


def shift(x, axis, by):
    n = lax.axis_size(axis)
    return lax.ppermute(x, axis, [(i, (i + by) % n) for i in range(n)])


def swap(x, axes):
    return lax.all_to_all(x, axes, 0, 0, tiled=True)


def body(queries, keys, values, out_grad, inputs, momentum, level_weight):
    length, width = queries.shape
    features = inputs.shape[1]
    n_y, n_z = lax.axis_size(Y), lax.axis_size(Z)
    heads = width // D
    sds = jax.ShapeDtypeStruct
    info = jnp.stack(
        [lax.axis_index(HEAD), lax.axis_index(Y), lax.axis_index(Z), jnp.int32(0)]
    ).astype(jnp.int32)

    square_sds = sds((length, width), bf16)
    held = pltpu.VMEM((length, width), bf16)
    dma = pltpu.SemaphoreType.DMA
    both = call(
        states_kernel,
        sds((heads, 2 * D, D), bf16),
        (queries, out_grad, keys, values),
        4 * length * width * D,
        [ANY] * 4,
        scratch=[held] * 4 + [dma((4,))],
        vmem=VMEM_ALL,
    )
    chunk = 512
    chunks = features // chunk
    local, *keyed = call(
        local_kernel,
        (sds((length, width), f32),) + tuple(sds((2, features, D), bf16) for _ in range(n_y)),
        (queries, keys, out_grad, inputs),
        4 * length * width * features + 3 * length * length * width,
        [ANY] * 4,
        (VMEM,) + (ANY,) * n_y,
        scratch=[held] * 3
        + [
            pltpu.VMEM((chunks, length, chunk), bf16),
            pltpu.VMEM((length, 2 * width), bf16),
            pltpu.VMEM((chunks, n_y, 2, chunk, D), bf16),
            dma((3 + chunks,)),
            dma((chunks, n_y)),
        ],
        scalars=(info, level_weight),
        vmem=VMEM_ALL,
    )
    both, *keyed[1:] = call(
        turn_kernel,
        sds((n_z, n_y, 2 * D // n_z, D), bf16),
        (swap(both, Y),),
        1 << 16,
        gated=keyed[1:],
        vmem=VMEM_ALL,
    )
    both = swap(both, Z)
    keyed = [keyed[0]] + [shift(keyed[n], Y, n) for n in range(1, n_y)]

    both = call(
        tree_kernel,
        sds(both.shape, bf16),
        (both,),
        1 << 21,
        scalars=(info, level_weight),
        vmem=8,
    )
    both = swap(both, Z)

    rows = features // 2
    parts, *own = call(
        project_kernel,
        (sds((n_z, features // n_z, D), bf16),)
        + tuple(sds((n_z, 2 * D // n_z, D), bf16) for _ in range(n_y)),
        (*keyed, both),
        2 * features * n_y * D * D,
        [ANY] * (n_y + 1),
        (ANY,) * (n_y + 1),
        scratch=[
            pltpu.VMEM((2, n_y, 2, rows, D), bf16),
            pltpu.VMEM(both.shape, bf16),
            pltpu.VMEM((2, n_z, rows // n_z, D), bf16),
            dma((1,)),
            dma((2, n_y)),
            dma((2,)),
            dma((n_y,)),
        ],
        scalars=(info,),
        vmem=VMEM_ALL,
    )
    parts = swap(parts, Z)

    own = [own[0]] + [shift(own[n], Y, n) for n in range(1, n_y)]
    query_grad, key_grad, value_grad, end = call(
        outputs_kernel,
        (sds((length, width), bf16),) * 3 + (sds((8, D), f32),),
        (queries, keys, values, out_grad, local, *own),
        6 * length * length * width,
        scalars=(info, level_weight),
        vmem=VMEM_ALL,
    )

    near, rest = HEAD + (Y,), (Z,)
    rows = momentum.shape[0]
    square, shard = call(
        shard_kernel,
        (sds((lax.axis_size(near), 1, D), f32), sds((n_y, heads, rows, D), f32)),
        (parts,),
        1 << 20,
        scratch=[pltpu.VMEM((n_y * rows, D), f32)],
        scalars=(info,),
        after=(end,),
        vmem=8,
    )
    shard = lax.psum_scatter(
        shard.reshape(n_y * heads * rows, D), Y, scatter_dimension=0, tiled=True
    ).reshape(heads, rows, D)
    square = swap(square, near)
    total = call(
        stage_kernel, sds((lax.axis_size(rest), 1, D), f32), (square,), 1 << 16, vmem=8
    )
    total = swap(total, rest)
    new_momentum = call(
        final_kernel, sds(momentum.shape, f32), (momentum, shard, total), 1 << 16, vmem=8
    )
    return (query_grad, key_grad, value_grad, new_momentum)


def solution(mesh):
    torus = Mesh(mesh.devices.reshape(4, 2, 4, 16), HEAD + SEQ)
    tokens = P(SEQ, HEAD)
    return jax.shard_map(
        body,
        mesh=torus,
        in_specs=(tokens, tokens, tokens, tokens, P(SEQ, None), tokens, P()),
        out_specs=(tokens, tokens, tokens, tokens),
        check_vma=False,
    )
```

```python
import functools
import math

import jax
import jax.numpy as jnp
import numpy as np
from jax import lax
from jax.experimental import pallas as pl
from jax.experimental.pallas import tpu as pltpu
from jax.sharding import Mesh
from jax.sharding import PartitionSpec as P

D = 128
HEAD = ("head_0", "head_1")
Y = "seq_0"
Z = "seq_1"
SEQ = (Y, Z)

VMEM_ALL = 60

clip_norm = 1024.0
momentum_rate = 0.9

bf16 = jnp.bfloat16
f32 = jnp.float32


def dot(a, b, ca, cb):
    return lax.dot_general(a, b, (((ca,), (cb,)), ((), ())), preferred_element_type=f32)


VMEM = pl.BlockSpec(memory_space=pltpu.VMEM)
ANY = pl.BlockSpec(memory_space=pl.ANY)


def call(kernel, out_shape, operands, flops, in_specs=None, out_specs=None, grid=(), scratch=(), vmem=16, after=(), scalars=(), gated=()):
    leaves = jax.tree.leaves((operands, out_shape))
    n = len(scalars) + len(operands)
    skip = n + len(after) + len(gated)
    last = skip + len(jax.tree.leaves(out_shape))

    def run(*refs):
        kernel(*refs[:n], *refs[skip:last], *refs[last + len(gated) :])

    in_specs = list(in_specs or [None] * len(operands))
    in_specs = [VMEM if i is None else i for i in in_specs]
    if out_specs is None:
        out_specs = jax.tree.map(lambda _: VMEM, out_shape)
    anywhere = ANY
    aliases = {}
    if gated:
        first = len(jax.tree.leaves(out_shape))
        aliases = {n + len(after) + i: first + i for i in range(len(gated))}
        out_shape = (*jax.tree.leaves(out_shape), *(jax.ShapeDtypeStruct(x.shape, x.dtype) for x in gated))
        out_specs = (*jax.tree.leaves(out_specs), *(anywhere for _ in gated))
    return pl.pallas_call(
        run,
        out_shape=out_shape,
        grid_spec=pltpu.PrefetchScalarGridSpec(
            num_scalar_prefetch=len(scalars),
            grid=grid,
            in_specs=in_specs + [anywhere] * (len(after) + len(gated)),
            out_specs=out_specs,
            scratch_shapes=list(scratch),
        ),
        input_output_aliases=aliases,
        compiler_params=pltpu.CompilerParams(vmem_limit_bytes=vmem * 1024 * 1024),
        cost_estimate=pl.CostEstimate(
            flops=flops,
            bytes_accessed=sum(x.size * x.dtype.itemsize for x in leaves),
            transcendentals=0,
        ),
    )(*scalars, *operands, *after, *gated)


def lanes(block):
    if isinstance(block, int):
        return slice(block * D, (block + 1) * D)
    return pl.ds(pl.multiple_of(block * D, D), D)


def lam(level, head, weight_ref):
    factor = np.float32(2.0 ** (-0.5 * level) / (8.0 * math.sqrt(D)))
    return weight_ref[level, head].astype(f32) * factor


def diagonal(head, weight_ref, transposed):
    row = lax.broadcasted_iota(jnp.int32, (D, D), 0)
    col = lax.broadcasted_iota(jnp.int32, (D, D), 1)
    apart = jnp.bitwise_xor(row, col)
    out = jnp.full((D, D), lam(0, head, weight_ref), f32)
    for level in range(1, D.bit_length()):
        out = jnp.where(apart >= 1 << (level - 1), lam(level, head, weight_ref), out)
    keep = row <= col if transposed else col <= row
    return jnp.where(keep, out, f32(0.0))


def far(i, j, head, weight_ref):
    return lam(D.bit_length() - 1 + (i ^ j).bit_length(), head, weight_ref)


def weighted(scores, first, own, head, weight_ref, diag):
    count = scores.shape[1] // D
    parts = []
    for n in range(count):
        part = scores[:, n * D : (n + 1) * D]
        w = diag if first + n == own else far(first + n, own, head, weight_ref)
        parts.append((w * part).astype(bf16))
    return parts[0] if count == 1 else jnp.concatenate(parts, axis=1)


def start_all(pairs, sems):
    moves = [pltpu.make_async_copy(source, to, sems.at[i]) for i, (source, to) in enumerate(pairs)]
    for move in moves:
        move.start()
    return moves


def states_kernel(q_hbm, g_hbm, k_hbm, v_hbm, out_ref, q_ref, g_ref, k_ref, v_ref, sems):
    moves = start_all(
        [(q_hbm, q_ref), (g_hbm, g_ref), (k_hbm, k_ref), (v_hbm, v_ref)], sems
    )
    moves[0].wait()
    moves[1].wait()
    for h in range(out_ref.shape[0]):
        s = lanes(h)
        out_ref[h, :D, :] = dot(q_ref[:, s], g_ref[:, s], 0, 0).astype(bf16)
    moves[2].wait()
    moves[3].wait()
    for h in range(out_ref.shape[0]):
        s = lanes(h)
        out_ref[h, D:, :] = dot(k_ref[:, s], v_ref[:, s], 0, 0).astype(bf16)


def local_kernel(info_ref, weight_ref, q_hbm, k_hbm, g_hbm, x_hbm, *refs):
    out_hbm = refs[:-8]
    q_ref, k_ref, g_ref, x_ref, right_ref, done_ref, in_sems, out_sems = refs[-8:]
    n_y = len(out_hbm)
    chunks, _, chunk = x_ref.shape
    moves = start_all(
        [(k_hbm, k_ref), (q_hbm, q_ref), (g_hbm, g_ref)]
        + [(x_hbm.at[:, pl.ds(c * chunk, chunk)], x_ref.at[c]) for c in range(chunks)],
        in_sems,
    )
    for move in moves[:3]:
        move.wait()
    blocks = q_ref.shape[0] // D
    for n in range(n_y):
        h = lax.rem(info_ref[1] + n, n_y)
        s = lanes(h)
        head = info_ref[0] * n_y + h
        keys, query, grad = k_ref[:, s], q_ref[:, s], g_ref[:, s]
        right_ref[:, lanes(2 * n)] = keys
        diag = diagonal(head, weight_ref, True)
        for j in range(blocks):
            rows = slice(j * D, (j + 1) * D)
            scores = dot(keys[rows], query[j * D :], 1, 1)
            mixed = weighted(scores, j, j, head, weight_ref, diag)
            res = dot(mixed, grad[j * D :], 1, 0)
            right_ref[rows, lanes(2 * n + 1)] = res.astype(bf16)
    sent = []
    for c in range(chunks):
        moves[3 + c].wait()
        res = dot(x_ref[c], right_ref[...], 0, 0).astype(bf16)
        for n in range(n_y):
            done_ref[c, n, 0, :, :] = res[:, lanes(2 * n)]
            done_ref[c, n, 1, :, :] = res[:, lanes(2 * n + 1)]
        part = pl.ds(c * chunk, chunk)
        sent += start_all(
            [(done_ref.at[c, n], out_hbm[n].at[:, part, :]) for n in range(n_y)], out_sems.at[c]
        )
    for move in sent:
        move.wait()


def tree_kernel(info_ref, weight_ref, in_ref, out_ref):
    nz, ny = out_ref.shape[:2]
    count = in_ref.shape[0]
    depth = count.bit_length() - 1
    head = info_ref[0] * ny + info_ref[1]
    is_grad = info_ref[2] < nz // 2
    sums = [[in_ref[c].astype(f32) for c in range(count)]]
    for bit in range(depth - 1):
        last = sums[-1]
        sums.append([last[2 * b] + last[2 * b + 1] for b in range(len(last) // 2)])
    total = [jnp.zeros(in_ref.shape[1:], f32)]
    for bit in reversed(range(depth)):
        w = lam(D.bit_length() + 2 + bit, head, weight_ref)
        later = jnp.where(is_grad, w, f32(0.0))
        earlier = jnp.where(is_grad, f32(0.0), w)
        last = sums[bit]
        total = [
            total[b // 2] + (later * last[b + 1] if b % 2 == 0 else earlier * last[b - 1])
            for b in range(len(last))
        ]
    for c in range(count):
        out_ref[c % nz, c // nz] = total[c].astype(bf16)


def project_kernel(info_ref, a0, a1, a2, a3, r_hbm, out_hbm, *refs):
    own_hbm = refs[:-7]
    a_ref, r_ref, done_ref, r_sem, a_sems, out_sems, own_sems = refs[-7:]
    keyed = (a0, a1, a2, a3)
    n_y = len(keyed)
    chunks, _, _, rows, _ = a_ref.shape
    got = start_all([(r_hbm, r_ref)], r_sem)
    moves = []
    for c in range(chunks):
        part = pl.ds(c * rows, rows)
        moves.append(
            start_all(
                [(keyed[n].at[:, part, :], a_ref.at[c, n]) for n in range(n_y)], a_sems.at[c]
            )
        )
    y = info_ref[1]
    half = r_ref.shape[0] // 2
    nz = out_hbm.shape[0]
    each = out_hbm.shape[1] // n_y
    got[0].wait()
    states = [r_ref[:half, lax.rem(y + n_y - n, n_y)].reshape(D, D) for n in range(n_y)]
    states = jnp.concatenate(states, axis=0)
    sent = []
    for c in range(chunks):
        for move in moves[c]:
            move.wait()
        left = jnp.concatenate([a_ref[c, n, 0] for n in range(n_y)], axis=1)
        res = dot(left, states, 1, 0)
        for n in range(n_y):
            res = res + a_ref[c, n, 1].astype(f32)
        res = res.astype(bf16)
        inner = rows // (nz * each)
        for b in range(inner):
            for z in range(nz):
                done_ref[c, z, b * each : (b + 1) * each, :] = res[
                    (b * nz + z) * each : (b * nz + z + 1) * each, :
                ]
        sent += start_all(
            [(done_ref.at[c], out_hbm.at[:, pl.ds(c * inner * each, inner * each), :])],
            out_sems.at[pl.ds(c, 1)],
        )
    sent += start_all(
        [(r_ref.at[:, lax.rem(y + n, n_y)], own_hbm[n]) for n in range(n_y)], own_sems
    )
    for move in sent:
        move.wait()


def outputs_kernel(
    info_ref, weight_ref, q_ref, k_ref, v_ref, g_ref, r0, r1, r2, r3, dq_ref, dk_ref, dv_ref, end_ref
):
    states = (r0, r1, r2, r3)
    n_y = len(states)
    end_ref[...] = jnp.zeros_like(end_ref)
    blocks = q_ref.shape[0] // D
    for n in range(n_y):
        h = lax.rem(info_ref[1] + n_y - n, n_y)
        s = lanes(h)
        head = info_ref[0] * n_y + h
        both = states[n][...].reshape(2 * D, D)
        returned, carried = both[:D], both[D:]
        query, keys, values, grad = q_ref[:, s], k_ref[:, s], v_ref[:, s], g_ref[:, s]
        base_v = dot(keys, returned, 1, 0)
        base_k = dot(values, returned, 1, 1)
        base_q = dot(grad, carried, 1, 1)
        diag = diagonal(head, weight_ref, False)
        diag_t = diagonal(head, weight_ref, True)
        for i in range(blocks):
            rows = slice(i * D, (i + 1) * D)
            upto = (i + 1) * D
            before = dot(grad[rows], values[:upto], 1, 1)
            dmix = weighted(before, 0, i, head, weight_ref, diag)
            dq_ref[rows, s] = (base_q[rows] + dot(dmix, keys[:upto], 1, 0)).astype(bf16)
            later = dot(values[rows], grad[i * D :], 1, 1)
            dmix_t = weighted(later, i, i, head, weight_ref, diag_t)
            dk_ref[rows, s] = (base_k[rows] + dot(dmix_t, query[i * D :], 1, 0)).astype(bf16)
            scores = dot(keys[rows], query[i * D :], 1, 1)
            mixed_t = weighted(scores, i, i, head, weight_ref, diag_t)
            dv_ref[rows, s] = (base_v[rows] + dot(mixed_t, grad[i * D :], 1, 0)).astype(bf16)


def shard_kernel(info_ref, in_ref, square_ref, out_ref, total_ref):
    n_y, heads, rows = out_ref.shape[:3]
    total = in_ref[0].astype(f32)
    for z in range(1, in_ref.shape[0]):
        total = total + in_ref[z].astype(f32)
    total_ref[...] = total
    square = jnp.sum(jnp.sum(total * total, axis=0, keepdims=True), axis=1, keepdims=True)
    square_ref[...] = jnp.broadcast_to(square[None], square_ref.shape)
    out_ref[...] = jnp.zeros_like(out_ref)
    for y in range(n_y):
        out_ref[y, info_ref[1], :, :] = total_ref[y * rows : (y + 1) * rows, :]


def stage_kernel(square_ref, out_ref):
    square = jnp.sum(square_ref[...], axis=0, keepdims=True)
    out_ref[...] = jnp.broadcast_to(square, out_ref.shape)


def final_kernel(mom_ref, in_ref, total_ref, out_ref):
    total = jnp.sum(total_ref[...], axis=0)
    factor = jnp.minimum(f32(1.0), clip_norm / jnp.sqrt(total + 1e-06))
    for h in range(in_ref.shape[0]):
        s = lanes(h)
        out_ref[:, s] = momentum_rate * mom_ref[:, s] + factor * in_ref[h]


def shift(x, axis, by):
    n = lax.axis_size(axis)
    return lax.ppermute(x, axis, [(i, (i + by) % n) for i in range(n)])


def swap(x, axes):
    return lax.all_to_all(x, axes, 0, 0, tiled=True)


def body(queries, keys, values, out_grad, inputs, momentum, level_weight):
    length, width = queries.shape
    features = inputs.shape[1]
    n_y, n_z = lax.axis_size(Y), lax.axis_size(Z)
    heads = width // D
    sds = jax.ShapeDtypeStruct
    info = jnp.stack(
        [lax.axis_index(HEAD), lax.axis_index(Y), lax.axis_index(Z), jnp.int32(0)]
    ).astype(jnp.int32)

    square_sds = sds((length, width), bf16)
    held = pltpu.VMEM((length, width), bf16)
    dma = pltpu.SemaphoreType.DMA
    both = call(
        states_kernel,
        sds((heads, 2 * D, D), bf16),
        (queries, out_grad, keys, values),
        4 * length * width * D,
        [ANY] * 4,
        scratch=[held] * 4 + [dma((4,))],
        vmem=VMEM_ALL,
    )
    chunk = 512
    chunks = features // chunk
    keyed = call(
        local_kernel,
        tuple(sds((2, features, D), bf16) for _ in range(n_y)),
        (queries, keys, out_grad, inputs),
        4 * length * width * features + 3 * length * length * width,
        [ANY] * 4,
        (ANY,) * n_y,
        scratch=[held] * 3
        + [
            pltpu.VMEM((chunks, length, chunk), bf16),
            pltpu.VMEM((length, 2 * width), bf16),
            pltpu.VMEM((chunks, n_y, 2, chunk, D), bf16),
            dma((3 + chunks,)),
            dma((chunks, n_y)),
        ],
        scalars=(info, level_weight),
        vmem=VMEM_ALL,
    )
    slices = (n_y * n_z, 2 * D // n_z, D)
    both = swap(both.reshape(slices), SEQ)
    keyed = [keyed[0]] + [shift(keyed[n], Y, n) for n in range(1, n_y)]

    both = call(
        tree_kernel,
        sds((n_z, n_y) + slices[1:], bf16),
        (both,),
        1 << 21,
        scalars=(info, level_weight),
        vmem=8,
    )
    both = swap(both, Z)

    rows = features // 2
    parts, *own = call(
        project_kernel,
        (sds((n_z, features // n_z, D), bf16),)
        + tuple(sds((n_z, 2 * D // n_z, D), bf16) for _ in range(n_y)),
        (*keyed, both),
        2 * features * n_y * D * D,
        [ANY] * (n_y + 1),
        (ANY,) * (n_y + 1),
        scratch=[
            pltpu.VMEM((2, n_y, 2, rows, D), bf16),
            pltpu.VMEM(both.shape, bf16),
            pltpu.VMEM((2, n_z, rows // n_z, D), bf16),
            dma((1,)),
            dma((2, n_y)),
            dma((2,)),
            dma((n_y,)),
        ],
        scalars=(info,),
        vmem=VMEM_ALL,
    )
    parts = swap(parts, Z)

    own = [own[0]] + [shift(own[n], Y, n) for n in range(1, n_y)]
    query_grad, key_grad, value_grad, end = call(
        outputs_kernel,
        (sds((length, width), bf16),) * 3 + (sds((8, D), f32),),
        (queries, keys, values, out_grad, *own),
        6 * length * length * width,
        scalars=(info, level_weight),
        vmem=VMEM_ALL,
    )

    near, rest = HEAD + (Y,), (Z,)
    rows = momentum.shape[0]
    square, shard = call(
        shard_kernel,
        (sds((lax.axis_size(near), 1, D), f32), sds((n_y, heads, rows, D), f32)),
        (parts,),
        1 << 20,
        scratch=[pltpu.VMEM((n_y * rows, D), f32)],
        scalars=(info,),
        after=(end,),
        vmem=8,
    )
    shard = lax.psum_scatter(
        shard.reshape(n_y * heads * rows, D), Y, scatter_dimension=0, tiled=True
    ).reshape(heads, rows, D)
    square = swap(square, near)
    total = call(
        stage_kernel, sds((lax.axis_size(rest), 1, D), f32), (square,), 1 << 16, vmem=8
    )
    total = swap(total, rest)
    new_momentum = call(
        final_kernel, sds(momentum.shape, f32), (momentum, shard, total), 1 << 16, vmem=8
    )
    return (query_grad, key_grad, value_grad, new_momentum)


def solution(mesh):
    torus = Mesh(mesh.devices.reshape(4, 2, 4, 16), HEAD + SEQ)
    tokens = P(SEQ, HEAD)
    return jax.shard_map(
        body,
        mesh=torus,
        in_specs=(tokens, tokens, tokens, tokens, P(SEQ, None), tokens, P()),
        out_specs=(tokens, tokens, tokens, tokens),
        check_vma=False,
    )
```

```python
import functools
import math

import jax
import jax.numpy as jnp
import numpy as np
from jax import lax
from jax.experimental import pallas as pl
from jax.experimental.pallas import tpu as pltpu
from jax.sharding import Mesh
from jax.sharding import PartitionSpec as P

D = 128
HEAD = ("head_0", "head_1")
Y = "seq_0"
Z = "seq_1"
SEQ = (Y, Z)

VMEM_ALL = 60

clip_norm = 1024.0
momentum_rate = 0.9

bf16 = jnp.bfloat16
f32 = jnp.float32


def dot(a, b, ca, cb):
    return lax.dot_general(a, b, (((ca,), (cb,)), ((), ())), preferred_element_type=f32)


VMEM = pl.BlockSpec(memory_space=pltpu.VMEM)
ANY = pl.BlockSpec(memory_space=pl.ANY)


def call(kernel, out_shape, operands, flops, in_specs=None, out_specs=None, grid=(), scratch=(), vmem=16, after=(), scalars=(), gated=()):
    leaves = jax.tree.leaves((operands, out_shape))
    n = len(scalars) + len(operands)
    skip = n + len(after) + len(gated)
    last = skip + len(jax.tree.leaves(out_shape))

    def run(*refs):
        kernel(*refs[:n], *refs[skip:last], *refs[last + len(gated) :])

    in_specs = list(in_specs or [None] * len(operands))
    in_specs = [VMEM if i is None else i for i in in_specs]
    if out_specs is None:
        out_specs = jax.tree.map(lambda _: VMEM, out_shape)
    anywhere = ANY
    aliases = {}
    if gated:
        first = len(jax.tree.leaves(out_shape))
        aliases = {n + len(after) + i: first + i for i in range(len(gated))}
        out_shape = (*jax.tree.leaves(out_shape), *(jax.ShapeDtypeStruct(x.shape, x.dtype) for x in gated))
        out_specs = (*jax.tree.leaves(out_specs), *(anywhere for _ in gated))
    return pl.pallas_call(
        run,
        out_shape=out_shape,
        grid_spec=pltpu.PrefetchScalarGridSpec(
            num_scalar_prefetch=len(scalars),
            grid=grid,
            in_specs=in_specs + [anywhere] * (len(after) + len(gated)),
            out_specs=out_specs,
            scratch_shapes=list(scratch),
        ),
        input_output_aliases=aliases,
        compiler_params=pltpu.CompilerParams(vmem_limit_bytes=vmem * 1024 * 1024),
        cost_estimate=pl.CostEstimate(
            flops=flops,
            bytes_accessed=sum(x.size * x.dtype.itemsize for x in leaves),
            transcendentals=0,
        ),
    )(*scalars, *operands, *after, *gated)


def lanes(block):
    if isinstance(block, int):
        return slice(block * D, (block + 1) * D)
    return pl.ds(pl.multiple_of(block * D, D), D)


def lam(level, head, weight_ref):
    factor = np.float32(2.0 ** (-0.5 * level) / (8.0 * math.sqrt(D)))
    return weight_ref[level, head].astype(f32) * factor


def diagonal(head, weight_ref, transposed):
    row = lax.broadcasted_iota(jnp.int32, (D, D), 0)
    col = lax.broadcasted_iota(jnp.int32, (D, D), 1)
    apart = jnp.bitwise_xor(row, col)
    out = jnp.full((D, D), lam(0, head, weight_ref), f32)
    for level in range(1, D.bit_length()):
        out = jnp.where(apart >= 1 << (level - 1), lam(level, head, weight_ref), out)
    keep = row <= col if transposed else col <= row
    return jnp.where(keep, out, f32(0.0))


def far(i, j, head, weight_ref):
    return lam(D.bit_length() - 1 + (i ^ j).bit_length(), head, weight_ref)


def weighted(scores, first, own, head, weight_ref, diag):
    count = scores.shape[1] // D
    parts = []
    for n in range(count):
        part = scores[:, n * D : (n + 1) * D]
        w = diag if first + n == own else far(first + n, own, head, weight_ref)
        parts.append((w * part).astype(bf16))
    return parts[0] if count == 1 else jnp.concatenate(parts, axis=1)


def start_all(pairs, sems):
    moves = [pltpu.make_async_copy(source, to, sems.at[i]) for i, (source, to) in enumerate(pairs)]
    for move in moves:
        move.start()
    return moves


def states_kernel(q_hbm, g_hbm, k_hbm, v_hbm, out_ref, q_ref, g_ref, k_ref, v_ref, sems):
    moves = start_all(
        [(q_hbm, q_ref), (g_hbm, g_ref), (k_hbm, k_ref), (v_hbm, v_ref)], sems
    )
    moves[0].wait()
    moves[1].wait()
    for h in range(out_ref.shape[0]):
        s = lanes(h)
        out_ref[h, :D, :] = dot(q_ref[:, s], g_ref[:, s], 0, 0).astype(bf16)
    moves[2].wait()
    moves[3].wait()
    for h in range(out_ref.shape[0]):
        s = lanes(h)
        out_ref[h, D:, :] = dot(k_ref[:, s], v_ref[:, s], 0, 0).astype(bf16)


def local_kernel(info_ref, weight_ref, q_hbm, k_hbm, g_hbm, x_hbm, *refs):
    out_hbm = refs[:-8]
    q_ref, k_ref, g_ref, x_ref, right_ref, done_ref, in_sems, out_sems = refs[-8:]
    n_y = len(out_hbm)
    chunks, _, chunk = x_ref.shape
    moves = start_all(
        [(k_hbm, k_ref), (q_hbm, q_ref), (g_hbm, g_ref)]
        + [(x_hbm.at[:, pl.ds(c * chunk, chunk)], x_ref.at[c]) for c in range(chunks)],
        in_sems,
    )
    for move in moves[:3]:
        move.wait()
    blocks = q_ref.shape[0] // D
    for n in range(n_y):
        h = lax.rem(info_ref[1] + n, n_y)
        s = lanes(h)
        head = info_ref[0] * n_y + h
        keys, query, grad = k_ref[:, s], q_ref[:, s], g_ref[:, s]
        right_ref[:, lanes(2 * n)] = keys
        diag = diagonal(head, weight_ref, True)
        for j in range(blocks):
            rows = slice(j * D, (j + 1) * D)
            scores = dot(keys[rows], query[j * D :], 1, 1)
            mixed = weighted(scores, j, j, head, weight_ref, diag)
            res = dot(mixed, grad[j * D :], 1, 0)
            right_ref[rows, lanes(2 * n + 1)] = res.astype(bf16)
    sent = []
    for c in range(chunks):
        moves[3 + c].wait()
        res = dot(x_ref[c], right_ref[...], 0, 0).astype(bf16)
        for n in range(n_y):
            done_ref[c, n, 0, :, :] = res[:, lanes(2 * n)]
            done_ref[c, n, 1, :, :] = res[:, lanes(2 * n + 1)]
        part = pl.ds(c * chunk, chunk)
        sent += start_all(
            [(done_ref.at[c, n], out_hbm[n].at[:, part, :]) for n in range(n_y)], out_sems.at[c]
        )
    for move in sent:
        move.wait()


def tree_kernel(info_ref, weight_ref, in_ref, out_ref):
    nz, ny = out_ref.shape[:2]
    count = in_ref.shape[0]
    depth = count.bit_length() - 1
    head = info_ref[0] * ny + info_ref[1]
    is_grad = info_ref[2] < nz // 2
    sums = [[in_ref[c].astype(f32) for c in range(count)]]
    for bit in range(depth - 1):
        last = sums[-1]
        sums.append([last[2 * b] + last[2 * b + 1] for b in range(len(last) // 2)])
    total = [jnp.zeros(in_ref.shape[1:], f32)]
    for bit in reversed(range(depth)):
        w = lam(D.bit_length() + 2 + bit, head, weight_ref)
        later = jnp.where(is_grad, w, f32(0.0))
        earlier = jnp.where(is_grad, f32(0.0), w)
        last = sums[bit]
        total = [
            total[b // 2] + (later * last[b + 1] if b % 2 == 0 else earlier * last[b - 1])
            for b in range(len(last))
        ]
    for c in range(count):
        out_ref[c % nz, c // nz] = total[c].astype(bf16)


def project_kernel(info_ref, a0, a1, a2, a3, r_hbm, out_hbm, *refs):
    own_hbm = refs[:-7]
    a_ref, r_ref, done_ref, r_sem, a_sems, out_sems, own_sems = refs[-7:]
    keyed = (a0, a1, a2, a3)
    n_y = len(keyed)
    chunks, _, _, rows, _ = a_ref.shape
    got = start_all([(r_hbm, r_ref)], r_sem)
    moves = []
    for c in range(chunks):
        part = pl.ds(c * rows, rows)
        moves.append(
            start_all(
                [(keyed[n].at[:, part, :], a_ref.at[c, n]) for n in range(n_y)], a_sems.at[c]
            )
        )
    y = info_ref[1]
    half = r_ref.shape[0] // 2
    nz = out_hbm.shape[0]
    each = out_hbm.shape[1] // n_y
    got[0].wait()
    states = [r_ref[:half, lax.rem(y + n_y - n, n_y)].reshape(D, D) for n in range(n_y)]
    states = jnp.concatenate(states, axis=0)
    sent = []
    for c in range(chunks):
        for move in moves[c]:
            move.wait()
        left = jnp.concatenate([a_ref[c, n, 0] for n in range(n_y)], axis=1)
        res = dot(left, states, 1, 0)
        for n in range(n_y):
            res = res + a_ref[c, n, 1].astype(f32)
        res = res.astype(bf16)
        inner = rows // (nz * each)
        for b in range(inner):
            for z in range(nz):
                done_ref[c, z, b * each : (b + 1) * each, :] = res[
                    (b * nz + z) * each : (b * nz + z + 1) * each, :
                ]
        sent += start_all(
            [(done_ref.at[c], out_hbm.at[:, pl.ds(c * inner * each, inner * each), :])],
            out_sems.at[pl.ds(c, 1)],
        )
    sent += start_all(
        [(r_ref.at[:, lax.rem(y + n, n_y)], own_hbm[n]) for n in range(n_y)], own_sems
    )
    for move in sent:
        move.wait()


def outputs_kernel(
    info_ref, weight_ref, q_ref, k_ref, v_ref, g_ref, r0, r1, r2, r3, dq_ref, dk_ref, dv_ref, end_ref
):
    states = (r0, r1, r2, r3)
    n_y = len(states)
    end_ref[...] = jnp.zeros_like(end_ref)
    blocks = q_ref.shape[0] // D
    for n in range(n_y):
        h = lax.rem(info_ref[1] + n_y - n, n_y)
        s = lanes(h)
        head = info_ref[0] * n_y + h
        both = states[n][...].reshape(2 * D, D)
        returned, carried = both[:D], both[D:]
        query, keys, values, grad = q_ref[:, s], k_ref[:, s], v_ref[:, s], g_ref[:, s]
        base_v = dot(keys, returned, 1, 0)
        base_k = dot(values, returned, 1, 1)
        base_q = dot(grad, carried, 1, 1)
        diag = diagonal(head, weight_ref, False)
        diag_t = diagonal(head, weight_ref, True)
        for i in range(blocks):
            rows = slice(i * D, (i + 1) * D)
            upto = (i + 1) * D
            before = dot(grad[rows], values[:upto], 1, 1)
            dmix = weighted(before, 0, i, head, weight_ref, diag)
            dq_ref[rows, s] = (base_q[rows] + dot(dmix, keys[:upto], 1, 0)).astype(bf16)
            later = dot(values[rows], grad[i * D :], 1, 1)
            dmix_t = weighted(later, i, i, head, weight_ref, diag_t)
            dk_ref[rows, s] = (base_k[rows] + dot(dmix_t, query[i * D :], 1, 0)).astype(bf16)
            scores = dot(keys[rows], query[i * D :], 1, 1)
            mixed_t = weighted(scores, i, i, head, weight_ref, diag_t)
            dv_ref[rows, s] = (base_v[rows] + dot(mixed_t, grad[i * D :], 1, 0)).astype(bf16)


def shard_kernel(info_ref, in_ref, square_ref, out_ref, total_ref):
    n_y, heads, rows = out_ref.shape[:3]
    total = in_ref[0].astype(f32)
    for z in range(1, in_ref.shape[0]):
        total = total + in_ref[z].astype(f32)
    total_ref[...] = total
    square = jnp.sum(jnp.sum(total * total, axis=0, keepdims=True), axis=1, keepdims=True)
    square_ref[...] = jnp.broadcast_to(square[None], square_ref.shape)
    out_ref[...] = jnp.zeros_like(out_ref)
    for y in range(n_y):
        out_ref[y, info_ref[1], :, :] = total_ref[y * rows : (y + 1) * rows, :]


def stage_kernel(square_ref, out_ref):
    square = jnp.sum(square_ref[...], axis=0, keepdims=True)
    out_ref[...] = jnp.broadcast_to(square, out_ref.shape)


def final_kernel(mom_ref, in_ref, total_ref, out_ref):
    total = jnp.sum(total_ref[...], axis=0)
    factor = jnp.minimum(f32(1.0), clip_norm / jnp.sqrt(total + 1e-06))
    for h in range(in_ref.shape[0]):
        s = lanes(h)
        out_ref[:, s] = momentum_rate * mom_ref[:, s] + factor * in_ref[h]


def shift(x, axis, by):
    n = lax.axis_size(axis)
    return lax.ppermute(x, axis, [(i, (i + by) % n) for i in range(n)])


def swap(x, axes):
    return lax.all_to_all(x, axes, 0, 0, tiled=True)


def body(queries, keys, values, out_grad, inputs, momentum, level_weight):
    length, width = queries.shape
    features = inputs.shape[1]
    n_y, n_z = lax.axis_size(Y), lax.axis_size(Z)
    heads = width // D
    sds = jax.ShapeDtypeStruct
    info = jnp.stack(
        [lax.axis_index(HEAD), lax.axis_index(Y), lax.axis_index(Z), jnp.int32(0)]
    ).astype(jnp.int32)

    square_sds = sds((length, width), bf16)
    held = pltpu.VMEM((length, width), bf16)
    dma = pltpu.SemaphoreType.DMA
    both = call(
        states_kernel,
        sds((heads, 2 * D, D), bf16),
        (queries, out_grad, keys, values),
        4 * length * width * D,
        [ANY] * 4,
        scratch=[held] * 4 + [dma((4,))],
        vmem=VMEM_ALL,
    )
    chunk = 512
    chunks = features // chunk
    keyed = call(
        local_kernel,
        tuple(sds((2, features, D), bf16) for _ in range(n_y)),
        (queries, keys, out_grad, inputs),
        4 * length * width * features + 3 * length * length * width,
        [ANY] * 4,
        (ANY,) * n_y,
        scratch=[held] * 3
        + [
            pltpu.VMEM((chunks, length, chunk), bf16),
            pltpu.VMEM((length, 2 * width), bf16),
            pltpu.VMEM((chunks, n_y, 2, chunk, D), bf16),
            dma((3 + chunks,)),
            dma((chunks, n_y)),
        ],
        scalars=(info, level_weight),
        vmem=52,
    )
    slices = (n_y * n_z, 2 * D // n_z, D)
    both = swap(both.reshape(slices), SEQ)
    keyed = [keyed[0]] + [shift(keyed[n], Y, n) for n in range(1, n_y)]

    both = call(
        tree_kernel,
        sds((n_z, n_y) + slices[1:], bf16),
        (both,),
        1 << 21,
        scalars=(info, level_weight),
        vmem=8,
    )
    both = swap(both, Z)

    rows = features // 2
    parts, *own = call(
        project_kernel,
        (sds((n_z, features // n_z, D), bf16),)
        + tuple(sds((n_z, 2 * D // n_z, D), bf16) for _ in range(n_y)),
        (*keyed, both),
        2 * features * n_y * D * D,
        [ANY] * (n_y + 1),
        (ANY,) * (n_y + 1),
        scratch=[
            pltpu.VMEM((2, n_y, 2, rows, D), bf16),
            pltpu.VMEM(both.shape, bf16),
            pltpu.VMEM((2, n_z, rows // n_z, D), bf16),
            dma((1,)),
            dma((2, n_y)),
            dma((2,)),
            dma((n_y,)),
        ],
        scalars=(info,),
        vmem=VMEM_ALL,
    )
    parts = swap(parts, Z)

    own = [own[0]] + [shift(own[n], Y, n) for n in range(1, n_y)]
    query_grad, key_grad, value_grad, end = call(
        outputs_kernel,
        (sds((length, width), bf16),) * 3 + (sds((8, D), f32),),
        (queries, keys, values, out_grad, *own),
        6 * length * length * width,
        scalars=(info, level_weight),
        vmem=VMEM_ALL,
    )

    near, rest = SEQ, HEAD
    rows = momentum.shape[0]
    square, shard = call(
        shard_kernel,
        (sds((lax.axis_size(near), 1, D), f32), sds((n_y, heads, rows, D), f32)),
        (parts,),
        1 << 20,
        scratch=[pltpu.VMEM((n_y * rows, D), f32)],
        scalars=(info,),
        after=(end,),
        vmem=8,
    )
    shard = lax.psum_scatter(
        shard.reshape(n_y * heads * rows, D), Y, scatter_dimension=0, tiled=True
    ).reshape(heads, rows, D)
    square = swap(square, near)
    total = call(
        stage_kernel, sds((lax.axis_size(rest), 1, D), f32), (square,), 1 << 16, vmem=8
    )
    total = swap(total, rest)
    new_momentum = call(
        final_kernel, sds(momentum.shape, f32), (momentum, shard, total), 1 << 16, vmem=8
    )
    return (query_grad, key_grad, value_grad, new_momentum)


def solution(mesh):
    torus = Mesh(mesh.devices.reshape(4, 2, 4, 16), HEAD + SEQ)
    tokens = P(SEQ, HEAD)
    return jax.shard_map(
        body,
        mesh=torus,
        in_specs=(tokens, tokens, tokens, tokens, P(SEQ, None), tokens, P()),
        out_specs=(tokens, tokens, tokens, tokens),
        check_vma=False,
    )
```

```python
import functools
import math

import jax
import jax.numpy as jnp
import numpy as np
from jax import lax
from jax.experimental import pallas as pl
from jax.experimental.pallas import tpu as pltpu
from jax.sharding import Mesh
from jax.sharding import PartitionSpec as P

D = 128
HEAD = ("head_0", "head_1")
Y = "seq_0"
Z = "seq_1"
SEQ = (Y, Z)

VMEM_ALL = 60

clip_norm = 1024.0
momentum_rate = 0.9

bf16 = jnp.bfloat16
f32 = jnp.float32


def dot(a, b, ca, cb):
    return lax.dot_general(a, b, (((ca,), (cb,)), ((), ())), preferred_element_type=f32)


VMEM = pl.BlockSpec(memory_space=pltpu.VMEM)
ANY = pl.BlockSpec(memory_space=pl.ANY)


def call(kernel, out_shape, operands, flops, in_specs=None, out_specs=None, grid=(), scratch=(), vmem=16, after=(), scalars=(), gated=()):
    leaves = jax.tree.leaves((operands, out_shape))
    n = len(scalars) + len(operands)
    skip = n + len(after) + len(gated)
    last = skip + len(jax.tree.leaves(out_shape))

    def run(*refs):
        kernel(*refs[:n], *refs[skip:last], *refs[last + len(gated) :])

    in_specs = list(in_specs or [None] * len(operands))
    in_specs = [VMEM if i is None else i for i in in_specs]
    if out_specs is None:
        out_specs = jax.tree.map(lambda _: VMEM, out_shape)
    anywhere = ANY
    aliases = {}
    if gated:
        first = len(jax.tree.leaves(out_shape))
        aliases = {n + len(after) + i: first + i for i in range(len(gated))}
        out_shape = (*jax.tree.leaves(out_shape), *(jax.ShapeDtypeStruct(x.shape, x.dtype) for x in gated))
        out_specs = (*jax.tree.leaves(out_specs), *(anywhere for _ in gated))
    return pl.pallas_call(
        run,
        out_shape=out_shape,
        grid_spec=pltpu.PrefetchScalarGridSpec(
            num_scalar_prefetch=len(scalars),
            grid=grid,
            in_specs=in_specs + [anywhere] * (len(after) + len(gated)),
            out_specs=out_specs,
            scratch_shapes=list(scratch),
        ),
        input_output_aliases=aliases,
        compiler_params=pltpu.CompilerParams(vmem_limit_bytes=vmem * 1024 * 1024),
        cost_estimate=pl.CostEstimate(
            flops=flops,
            bytes_accessed=sum(x.size * x.dtype.itemsize for x in leaves),
            transcendentals=0,
        ),
    )(*scalars, *operands, *after, *gated)


def lanes(block):
    if isinstance(block, int):
        return slice(block * D, (block + 1) * D)
    return pl.ds(pl.multiple_of(block * D, D), D)


def lam(level, head, weight_ref):
    factor = np.float32(2.0 ** (-0.5 * level) / (8.0 * math.sqrt(D)))
    return weight_ref[level, head].astype(f32) * factor


def diagonal(head, weight_ref, transposed):
    row = lax.broadcasted_iota(jnp.int32, (D, D), 0)
    col = lax.broadcasted_iota(jnp.int32, (D, D), 1)
    apart = jnp.bitwise_xor(row, col)
    out = jnp.full((D, D), lam(0, head, weight_ref), f32)
    for level in range(1, D.bit_length()):
        out = jnp.where(apart >= 1 << (level - 1), lam(level, head, weight_ref), out)
    keep = row <= col if transposed else col <= row
    return jnp.where(keep, out, f32(0.0))


def far(i, j, head, weight_ref):
    return lam(D.bit_length() - 1 + (i ^ j).bit_length(), head, weight_ref)


def weighted(scores, first, own, head, weight_ref, diag):
    count = scores.shape[1] // D
    parts = []
    for n in range(count):
        part = scores[:, n * D : (n + 1) * D]
        w = diag if first + n == own else far(first + n, own, head, weight_ref)
        parts.append((w * part).astype(bf16))
    return parts[0] if count == 1 else jnp.concatenate(parts, axis=1)


def start_all(pairs, sems):
    moves = [pltpu.make_async_copy(source, to, sems.at[i]) for i, (source, to) in enumerate(pairs)]
    for move in moves:
        move.start()
    return moves


def states_kernel(q_hbm, g_hbm, k_hbm, v_hbm, out_ref, q_ref, g_ref, k_ref, v_ref, sems):
    moves = start_all(
        [(q_hbm, q_ref), (g_hbm, g_ref), (k_hbm, k_ref), (v_hbm, v_ref)], sems
    )
    moves[0].wait()
    moves[1].wait()
    for h in range(out_ref.shape[0]):
        s = lanes(h)
        out_ref[h, :D, :] = dot(q_ref[:, s], g_ref[:, s], 0, 0).astype(bf16)
    moves[2].wait()
    moves[3].wait()
    for h in range(out_ref.shape[0]):
        s = lanes(h)
        out_ref[h, D:, :] = dot(k_ref[:, s], v_ref[:, s], 0, 0).astype(bf16)


def local_kernel(info_ref, weight_ref, q_hbm, k_hbm, g_hbm, x_hbm, *refs):
    out_hbm = refs[:-8]
    q_ref, k_ref, g_ref, x_ref, right_ref, done_ref, in_sems, out_sems = refs[-8:]
    n_y = len(out_hbm)
    chunks, _, chunk = x_ref.shape
    moves = start_all(
        [(k_hbm, k_ref), (q_hbm, q_ref), (g_hbm, g_ref)]
        + [(x_hbm.at[:, pl.ds(c * chunk, chunk)], x_ref.at[c]) for c in range(chunks)],
        in_sems,
    )
    for move in moves[:3]:
        move.wait()
    blocks = q_ref.shape[0] // D
    for n in range(n_y):
        h = lax.rem(info_ref[1] + n, n_y)
        s = lanes(h)
        head = info_ref[0] * n_y + h
        keys, query, grad = k_ref[:, s], q_ref[:, s], g_ref[:, s]
        right_ref[:, lanes(2 * n)] = keys
        diag = diagonal(head, weight_ref, True)
        for j in range(blocks):
            rows = slice(j * D, (j + 1) * D)
            scores = dot(keys[rows], query[j * D :], 1, 1)
            mixed = weighted(scores, j, j, head, weight_ref, diag)
            res = dot(mixed, grad[j * D :], 1, 0)
            right_ref[rows, lanes(2 * n + 1)] = res.astype(bf16)
    sent = []
    for c in range(chunks):
        moves[3 + c].wait()
        res = dot(x_ref[c], right_ref[...], 0, 0).astype(bf16)
        for n in range(n_y):
            done_ref[c, n, 0, :, :] = res[:, lanes(2 * n)]
            done_ref[c, n, 1, :, :] = res[:, lanes(2 * n + 1)]
        part = pl.ds(c * chunk, chunk)
        sent += start_all(
            [(done_ref.at[c, n], out_hbm[n].at[:, part, :]) for n in range(n_y)], out_sems.at[c]
        )
    for move in sent:
        move.wait()


def tree_kernel(info_ref, weight_ref, in_ref, out_ref):
    nz, ny = out_ref.shape[:2]
    count = in_ref.shape[0]
    depth = count.bit_length() - 1
    head = info_ref[0] * ny + info_ref[1]
    is_grad = info_ref[2] < nz // 2
    sums = [[in_ref[c].astype(f32) for c in range(count)]]
    for bit in range(depth - 1):
        last = sums[-1]
        sums.append([last[2 * b] + last[2 * b + 1] for b in range(len(last) // 2)])
    total = [jnp.zeros(in_ref.shape[1:], f32)]
    for bit in reversed(range(depth)):
        w = lam(D.bit_length() + 2 + bit, head, weight_ref)
        later = jnp.where(is_grad, w, f32(0.0))
        earlier = jnp.where(is_grad, f32(0.0), w)
        last = sums[bit]
        total = [
            total[b // 2] + (later * last[b + 1] if b % 2 == 0 else earlier * last[b - 1])
            for b in range(len(last))
        ]
    for c in range(count):
        out_ref[c % nz, c // nz] = total[c].astype(bf16)


def project_kernel(info_ref, a0, a1, a2, a3, r_hbm, out_hbm, *refs):
    own_hbm = refs[:-7]
    a_ref, r_ref, done_ref, r_sem, a_sems, out_sems, own_sems = refs[-7:]
    keyed = (a0, a1, a2, a3)
    n_y = len(keyed)
    chunks, _, _, rows, _ = a_ref.shape
    got = start_all([(r_hbm, r_ref)], r_sem)
    moves = []
    for c in range(chunks):
        part = pl.ds(c * rows, rows)
        moves.append(
            start_all(
                [(keyed[n].at[:, part, :], a_ref.at[c, n]) for n in range(n_y)], a_sems.at[c]
            )
        )
    y = info_ref[1]
    half = r_ref.shape[0] // 2
    nz = out_hbm.shape[0]
    each = out_hbm.shape[1] // n_y
    got[0].wait()
    states = [r_ref[:half, lax.rem(y + n_y - n, n_y)].reshape(D, D) for n in range(n_y)]
    states = jnp.concatenate(states, axis=0)
    sent = []
    for c in range(chunks):
        for move in moves[c]:
            move.wait()
        left = jnp.concatenate([a_ref[c, n, 0] for n in range(n_y)], axis=1)
        res = dot(left, states, 1, 0)
        for n in range(n_y):
            res = res + a_ref[c, n, 1].astype(f32)
        res = res.astype(bf16)
        inner = rows // (nz * each)
        for b in range(inner):
            for z in range(nz):
                done_ref[c, z, b * each : (b + 1) * each, :] = res[
                    (b * nz + z) * each : (b * nz + z + 1) * each, :
                ]
        sent += start_all(
            [(done_ref.at[c], out_hbm.at[:, pl.ds(c * inner * each, inner * each), :])],
            out_sems.at[pl.ds(c, 1)],
        )
    sent += start_all(
        [(r_ref.at[:, lax.rem(y + n, n_y)], own_hbm[n]) for n in range(n_y)], own_sems
    )
    for move in sent:
        move.wait()


def outputs_kernel(
    info_ref, weight_ref, q_ref, k_ref, v_ref, g_ref, r0, r1, r2, r3, dq_ref, dk_ref, dv_ref, end_ref
):
    states = (r0, r1, r2, r3)
    n_y = len(states)
    end_ref[...] = jnp.zeros_like(end_ref)
    blocks = q_ref.shape[0] // D
    for n in range(n_y):
        h = lax.rem(info_ref[1] + n_y - n, n_y)
        s = lanes(h)
        head = info_ref[0] * n_y + h
        both = states[n][...].reshape(2 * D, D)
        returned, carried = both[:D], both[D:]
        query, keys, values, grad = q_ref[:, s], k_ref[:, s], v_ref[:, s], g_ref[:, s]
        base_v = dot(keys, returned, 1, 0)
        base_k = dot(values, returned, 1, 1)
        base_q = dot(grad, carried, 1, 1)
        diag = diagonal(head, weight_ref, False)
        diag_t = diagonal(head, weight_ref, True)
        for i in range(blocks):
            rows = slice(i * D, (i + 1) * D)
            upto = (i + 1) * D
            before = dot(grad[rows], values[:upto], 1, 1)
            dmix = weighted(before, 0, i, head, weight_ref, diag)
            dq_ref[rows, s] = (base_q[rows] + dot(dmix, keys[:upto], 1, 0)).astype(bf16)
            later = dot(values[rows], grad[i * D :], 1, 1)
            dmix_t = weighted(later, i, i, head, weight_ref, diag_t)
            dk_ref[rows, s] = (base_k[rows] + dot(dmix_t, query[i * D :], 1, 0)).astype(bf16)
            scores = dot(keys[rows], query[i * D :], 1, 1)
            mixed_t = weighted(scores, i, i, head, weight_ref, diag_t)
            dv_ref[rows, s] = (base_v[rows] + dot(mixed_t, grad[i * D :], 1, 0)).astype(bf16)


def shard_kernel(info_ref, in_ref, square_ref, out_ref, total_ref):
    n_y, heads, rows = out_ref.shape[:3]
    total = in_ref[0].astype(f32)
    for z in range(1, in_ref.shape[0]):
        total = total + in_ref[z].astype(f32)
    total_ref[...] = total
    square = jnp.sum(jnp.sum(total * total, axis=0, keepdims=True), axis=1, keepdims=True)
    square_ref[...] = jnp.broadcast_to(square[None], square_ref.shape)
    out_ref[...] = jnp.zeros_like(out_ref)
    for y in range(n_y):
        out_ref[y, info_ref[1], :, :] = total_ref[y * rows : (y + 1) * rows, :]


def stage_kernel(square_ref, out_ref):
    square = jnp.sum(square_ref[...], axis=0, keepdims=True)
    out_ref[...] = jnp.broadcast_to(square, out_ref.shape)


def final_kernel(mom_ref, in_ref, total_ref, out_ref):
    total = jnp.sum(total_ref[...], axis=0)
    factor = jnp.minimum(f32(1.0), clip_norm / jnp.sqrt(total + 1e-06))
    for h in range(in_ref.shape[0]):
        s = lanes(h)
        out_ref[:, s] = momentum_rate * mom_ref[:, s] + factor * in_ref[h]


def shift(x, axis, by):
    n = lax.axis_size(axis)
    return lax.ppermute(x, axis, [(i, (i + by) % n) for i in range(n)])


def swap(x, axes):
    return lax.all_to_all(x, axes, 0, 0, tiled=True)


def body(queries, keys, values, out_grad, inputs, momentum, level_weight):
    length, width = queries.shape
    features = inputs.shape[1]
    n_y, n_z = lax.axis_size(Y), lax.axis_size(Z)
    heads = width // D
    sds = jax.ShapeDtypeStruct
    info = jnp.stack(
        [lax.axis_index(HEAD), lax.axis_index(Y), lax.axis_index(Z), jnp.int32(0)]
    ).astype(jnp.int32)

    square_sds = sds((length, width), bf16)
    held = pltpu.VMEM((length, width), bf16)
    dma = pltpu.SemaphoreType.DMA
    both = call(
        states_kernel,
        sds((heads, 2 * D, D), bf16),
        (queries, out_grad, keys, values),
        4 * length * width * D,
        [ANY] * 4,
        scratch=[held] * 4 + [dma((4,))],
        vmem=VMEM_ALL,
    )
    chunk = 512
    chunks = features // chunk
    keyed = call(
        local_kernel,
        tuple(sds((2, features, D), bf16) for _ in range(n_y)),
        (queries, keys, out_grad, inputs),
        4 * length * width * features + 3 * length * length * width,
        [ANY] * 4,
        (ANY,) * n_y,
        scratch=[held] * 3
        + [
            pltpu.VMEM((chunks, length, chunk), bf16),
            pltpu.VMEM((length, 2 * width), bf16),
            pltpu.VMEM((chunks, n_y, 2, chunk, D), bf16),
            dma((3 + chunks,)),
            dma((chunks, n_y)),
        ],
        scalars=(info, level_weight),
        vmem=52,
    )
    slices = (n_y * n_z, 2 * D // n_z, D)
    both = swap(both.reshape(slices), SEQ)
    gone = {n: shift(keyed[n], Y, n) for n in sorted(range(1, n_y), key=lambda n: abs(n - n_y // 2))}
    keyed = [keyed[0]] + [gone[n] for n in range(1, n_y)]

    both = call(
        tree_kernel,
        sds((n_z, n_y) + slices[1:], bf16),
        (both,),
        1 << 21,
        scalars=(info, level_weight),
        vmem=8,
    )
    both = swap(both, Z)

    rows = features // 2
    parts, *own = call(
        project_kernel,
        (sds((n_z, features // n_z, D), bf16),)
        + tuple(sds((n_z, 2 * D // n_z, D), bf16) for _ in range(n_y)),
        (*keyed, both),
        2 * features * n_y * D * D,
        [ANY] * (n_y + 1),
        (ANY,) * (n_y + 1),
        scratch=[
            pltpu.VMEM((2, n_y, 2, rows, D), bf16),
            pltpu.VMEM(both.shape, bf16),
            pltpu.VMEM((2, n_z, rows // n_z, D), bf16),
            dma((1,)),
            dma((2, n_y)),
            dma((2,)),
            dma((n_y,)),
        ],
        scalars=(info,),
        vmem=52,
    )
    parts = swap(parts, Z)

    own = [own[0]] + [shift(own[n], Y, n) for n in range(1, n_y)]
    query_grad, key_grad, value_grad, end = call(
        outputs_kernel,
        (sds((length, width), bf16),) * 3 + (sds((8, D), f32),),
        (queries, keys, values, out_grad, *own),
        6 * length * length * width,
        scalars=(info, level_weight),
        vmem=52,
    )

    near, rest = HEAD + (Y,), (Z,)
    rows = momentum.shape[0]
    square, shard = call(
        shard_kernel,
        (sds((lax.axis_size(near), 1, D), f32), sds((n_y, heads, rows, D), f32)),
        (parts,),
        1 << 20,
        scratch=[pltpu.VMEM((n_y * rows, D), f32)],
        scalars=(info,),
        after=(end,),
        vmem=8,
    )
    shard = lax.psum_scatter(
        shard.reshape(n_y * heads * rows, D), Y, scatter_dimension=0, tiled=True
    ).reshape(heads, rows, D)
    square = swap(square, near)
    total = call(
        stage_kernel, sds((lax.axis_size(rest), 1, D), f32), (square,), 1 << 16, vmem=8
    )
    total = swap(total, rest)
    new_momentum = call(
        final_kernel, sds(momentum.shape, f32), (momentum, shard, total), 1 << 16, vmem=8
    )
    return (query_grad, key_grad, value_grad, new_momentum)


def solution(mesh):
    torus = Mesh(mesh.devices.reshape(4, 2, 4, 16), HEAD + SEQ)
    tokens = P(SEQ, HEAD)
    return jax.shard_map(
        body,
        mesh=torus,
        in_specs=(tokens, tokens, tokens, tokens, P(SEQ, None), tokens, P()),
        out_specs=(tokens, tokens, tokens, tokens),
        check_vma=False,
    )
```

```python
import functools
import math

import jax
import jax.numpy as jnp
import numpy as np
from jax import lax
from jax.experimental import pallas as pl
from jax.experimental.pallas import tpu as pltpu
from jax.sharding import Mesh
from jax.sharding import PartitionSpec as P

D = 128
HEAD = ("head_0", "head_1")
Y = "seq_0"
Z = "seq_1"
SEQ = (Y, Z)

VMEM_ALL = 60

clip_norm = 1024.0
momentum_rate = 0.9

bf16 = jnp.bfloat16
f32 = jnp.float32


def dot(a, b, ca, cb):
    return lax.dot_general(a, b, (((ca,), (cb,)), ((), ())), preferred_element_type=f32)


VMEM = pl.BlockSpec(memory_space=pltpu.VMEM)
ANY = pl.BlockSpec(memory_space=pl.ANY)


def call(kernel, out_shape, operands, flops, in_specs=None, out_specs=None, grid=(), scratch=(), vmem=16, after=(), scalars=(), gated=()):
    leaves = jax.tree.leaves((operands, out_shape))
    n = len(scalars) + len(operands)
    skip = n + len(after) + len(gated)
    last = skip + len(jax.tree.leaves(out_shape))

    def run(*refs):
        kernel(*refs[:n], *refs[skip:last], *refs[last + len(gated) :])

    in_specs = list(in_specs or [None] * len(operands))
    in_specs = [VMEM if i is None else i for i in in_specs]
    if out_specs is None:
        out_specs = jax.tree.map(lambda _: VMEM, out_shape)
    anywhere = ANY
    aliases = {}
    if gated:
        first = len(jax.tree.leaves(out_shape))
        aliases = {n + len(after) + i: first + i for i in range(len(gated))}
        out_shape = (*jax.tree.leaves(out_shape), *(jax.ShapeDtypeStruct(x.shape, x.dtype) for x in gated))
        out_specs = (*jax.tree.leaves(out_specs), *(anywhere for _ in gated))
    return pl.pallas_call(
        run,
        out_shape=out_shape,
        grid_spec=pltpu.PrefetchScalarGridSpec(
            num_scalar_prefetch=len(scalars),
            grid=grid,
            in_specs=in_specs + [anywhere] * (len(after) + len(gated)),
            out_specs=out_specs,
            scratch_shapes=list(scratch),
        ),
        input_output_aliases=aliases,
        compiler_params=pltpu.CompilerParams(vmem_limit_bytes=vmem * 1024 * 1024),
        cost_estimate=pl.CostEstimate(
            flops=flops,
            bytes_accessed=sum(x.size * x.dtype.itemsize for x in leaves),
            transcendentals=0,
        ),
    )(*scalars, *operands, *after, *gated)


def lanes(block):
    if isinstance(block, int):
        return slice(block * D, (block + 1) * D)
    return pl.ds(pl.multiple_of(block * D, D), D)


def lam(level, head, weight_ref):
    factor = np.float32(2.0 ** (-0.5 * level) / (8.0 * math.sqrt(D)))
    return weight_ref[level, head].astype(f32) * factor


def diagonal(head, weight_ref, transposed):
    row = lax.broadcasted_iota(jnp.int32, (D, D), 0)
    col = lax.broadcasted_iota(jnp.int32, (D, D), 1)
    apart = jnp.bitwise_xor(row, col)
    out = jnp.full((D, D), lam(0, head, weight_ref), f32)
    for level in range(1, D.bit_length()):
        out = jnp.where(apart >= 1 << (level - 1), lam(level, head, weight_ref), out)
    keep = row <= col if transposed else col <= row
    return jnp.where(keep, out, f32(0.0))


def far(i, j, head, weight_ref):
    return lam(D.bit_length() - 1 + (i ^ j).bit_length(), head, weight_ref)


def weighted(scores, first, own, head, weight_ref, diag):
    count = scores.shape[1] // D
    parts = []
    for n in range(count):
        part = scores[:, n * D : (n + 1) * D]
        w = diag if first + n == own else far(first + n, own, head, weight_ref)
        parts.append((w * part).astype(bf16))
    return parts[0] if count == 1 else jnp.concatenate(parts, axis=1)


def start_all(pairs, sems):
    moves = [pltpu.make_async_copy(source, to, sems.at[i]) for i, (source, to) in enumerate(pairs)]
    for move in moves:
        move.start()
    return moves


def states_kernel(q_hbm, g_hbm, k_hbm, v_hbm, out_ref, q_ref, g_ref, k_ref, v_ref, sems):
    moves = start_all(
        [(q_hbm, q_ref), (g_hbm, g_ref), (k_hbm, k_ref), (v_hbm, v_ref)], sems
    )
    moves[0].wait()
    moves[1].wait()
    for h in range(out_ref.shape[0]):
        s = lanes(h)
        out_ref[h, :D, :] = dot(q_ref[:, s], g_ref[:, s], 0, 0).astype(bf16)
    moves[2].wait()
    moves[3].wait()
    for h in range(out_ref.shape[0]):
        s = lanes(h)
        out_ref[h, D:, :] = dot(k_ref[:, s], v_ref[:, s], 0, 0).astype(bf16)


def local_kernel(info_ref, weight_ref, q_hbm, k_hbm, g_hbm, x_hbm, *refs):
    out_hbm = refs[:-8]
    q_ref, k_ref, g_ref, x_ref, right_ref, done_ref, in_sems, out_sems = refs[-8:]
    n_y = len(out_hbm)
    chunks, _, chunk = x_ref.shape
    moves = start_all(
        [(k_hbm, k_ref), (q_hbm, q_ref), (g_hbm, g_ref)]
        + [(x_hbm.at[:, pl.ds(c * chunk, chunk)], x_ref.at[c]) for c in range(chunks)],
        in_sems,
    )
    for move in moves[:3]:
        move.wait()
    blocks = q_ref.shape[0] // D
    for n in range(n_y):
        h = lax.rem(info_ref[1] + n, n_y)
        s = lanes(h)
        head = info_ref[0] * n_y + h
        keys, query, grad = k_ref[:, s], q_ref[:, s], g_ref[:, s]
        right_ref[:, lanes(2 * n)] = keys
        diag = diagonal(head, weight_ref, True)
        for j in range(blocks):
            rows = slice(j * D, (j + 1) * D)
            scores = dot(keys[rows], query[j * D :], 1, 1)
            mixed = weighted(scores, j, j, head, weight_ref, diag)
            res = dot(mixed, grad[j * D :], 1, 0)
            right_ref[rows, lanes(2 * n + 1)] = res.astype(bf16)
    sent = []
    for c in range(chunks):
        moves[3 + c].wait()
        res = dot(x_ref[c], right_ref[...], 0, 0).astype(bf16)
        for n in range(n_y):
            done_ref[c, n, 0, :, :] = res[:, lanes(2 * n)]
            done_ref[c, n, 1, :, :] = res[:, lanes(2 * n + 1)]
        part = pl.ds(c * chunk, chunk)
        sent += start_all(
            [(done_ref.at[c, n], out_hbm[n].at[:, part, :]) for n in range(n_y)], out_sems.at[c]
        )
    for move in sent:
        move.wait()


def tree_kernel(info_ref, weight_ref, in_ref, out_ref):
    nz, ny = out_ref.shape[:2]
    count = in_ref.shape[0]
    depth = count.bit_length() - 1
    head = info_ref[0] * ny + info_ref[1]
    is_grad = info_ref[2] < nz // 2
    sums = [[in_ref[c].astype(f32) for c in range(count)]]
    for bit in range(depth - 1):
        last = sums[-1]
        sums.append([last[2 * b] + last[2 * b + 1] for b in range(len(last) // 2)])
    total = [jnp.zeros(in_ref.shape[1:], f32)]
    for bit in reversed(range(depth)):
        w = lam(D.bit_length() + 2 + bit, head, weight_ref)
        later = jnp.where(is_grad, w, f32(0.0))
        earlier = jnp.where(is_grad, f32(0.0), w)
        last = sums[bit]
        total = [
            total[b // 2] + (later * last[b + 1] if b % 2 == 0 else earlier * last[b - 1])
            for b in range(len(last))
        ]
    for c in range(count):
        out_ref[c % nz, c // nz] = total[c].astype(bf16)


def project_kernel(info_ref, a0, a1, a2, a3, r_hbm, out_hbm, *refs):
    own_hbm = refs[:-7]
    a_ref, r_ref, done_ref, r_sem, a_sems, out_sems, own_sems = refs[-7:]
    keyed = (a0, a1, a2, a3)
    n_y = len(keyed)
    chunks, _, _, rows, _ = a_ref.shape
    got = start_all([(r_hbm, r_ref)], r_sem)
    moves = []
    for c in range(chunks):
        part = pl.ds(c * rows, rows)
        moves.append(
            start_all(
                [(keyed[n].at[:, part, :], a_ref.at[c, n]) for n in range(n_y)], a_sems.at[c]
            )
        )
    y = info_ref[1]
    half = r_ref.shape[0] // 2
    nz = out_hbm.shape[0]
    each = out_hbm.shape[1] // n_y
    got[0].wait()
    states = [r_ref[:half, lax.rem(y + n_y - n, n_y)].reshape(D, D) for n in range(n_y)]
    states = jnp.concatenate(states, axis=0)
    sent = []
    for c in range(chunks):
        for move in moves[c]:
            move.wait()
        left = jnp.concatenate([a_ref[c, n, 0] for n in range(n_y)], axis=1)
        res = dot(left, states, 1, 0)
        for n in range(n_y):
            res = res + a_ref[c, n, 1].astype(f32)
        res = res.astype(bf16)
        inner = rows // (nz * each)
        for b in range(inner):
            for z in range(nz):
                done_ref[c, z, b * each : (b + 1) * each, :] = res[
                    (b * nz + z) * each : (b * nz + z + 1) * each, :
                ]
        sent += start_all(
            [(done_ref.at[c], out_hbm.at[:, pl.ds(c * inner * each, inner * each), :])],
            out_sems.at[pl.ds(c, 1)],
        )
    sent += start_all(
        [(r_ref.at[:, lax.rem(y + n, n_y)], own_hbm[n]) for n in range(n_y)], own_sems
    )
    for move in sent:
        move.wait()


def outputs_kernel(
    info_ref, weight_ref, q_ref, k_ref, v_ref, g_ref, r0, r1, r2, r3, dq_ref, dk_ref, dv_ref, end_ref
):
    states = (r0, r1, r2, r3)
    n_y = len(states)
    end_ref[...] = jnp.zeros_like(end_ref)
    blocks = q_ref.shape[0] // D
    for n in range(n_y):
        h = lax.rem(info_ref[1] + n_y - n, n_y)
        s = lanes(h)
        head = info_ref[0] * n_y + h
        both = states[n][...].reshape(2 * D, D)
        returned, carried = both[:D], both[D:]
        query, keys, values, grad = q_ref[:, s], k_ref[:, s], v_ref[:, s], g_ref[:, s]
        base_v = dot(keys, returned, 1, 0)
        base_k = dot(values, returned, 1, 1)
        base_q = dot(grad, carried, 1, 1)
        diag = diagonal(head, weight_ref, False)
        diag_t = diagonal(head, weight_ref, True)
        for i in range(blocks):
            rows = slice(i * D, (i + 1) * D)
            upto = (i + 1) * D
            before = dot(grad[rows], values[:upto], 1, 1)
            dmix = weighted(before, 0, i, head, weight_ref, diag)
            dq_ref[rows, s] = (base_q[rows] + dot(dmix, keys[:upto], 1, 0)).astype(bf16)
            later = dot(values[rows], grad[i * D :], 1, 1)
            dmix_t = weighted(later, i, i, head, weight_ref, diag_t)
            dk_ref[rows, s] = (base_k[rows] + dot(dmix_t, query[i * D :], 1, 0)).astype(bf16)
            scores = dot(keys[rows], query[i * D :], 1, 1)
            mixed_t = weighted(scores, i, i, head, weight_ref, diag_t)
            dv_ref[rows, s] = (base_v[rows] + dot(mixed_t, grad[i * D :], 1, 0)).astype(bf16)


def shard_kernel(info_ref, in_ref, square_ref, out_ref, total_ref):
    n_y, heads, rows = out_ref.shape[:3]
    total = in_ref[0].astype(f32)
    for z in range(1, in_ref.shape[0]):
        total = total + in_ref[z].astype(f32)
    total_ref[...] = total
    square = jnp.sum(jnp.sum(total * total, axis=0, keepdims=True), axis=1, keepdims=True)
    square_ref[...] = jnp.broadcast_to(square[None], square_ref.shape)
    out_ref[...] = jnp.zeros_like(out_ref)
    for y in range(n_y):
        out_ref[y, info_ref[1], :, :] = total_ref[y * rows : (y + 1) * rows, :]


def stage_kernel(square_ref, out_ref):
    square = jnp.sum(square_ref[...], axis=0, keepdims=True)
    out_ref[...] = jnp.broadcast_to(square, out_ref.shape)


def final_kernel(mom_ref, in_ref, total_ref, out_ref):
    total = jnp.sum(total_ref[...], axis=0)
    factor = jnp.minimum(f32(1.0), clip_norm / jnp.sqrt(total + 1e-06))
    for h in range(in_ref.shape[0]):
        s = lanes(h)
        out_ref[:, s] = momentum_rate * mom_ref[:, s] + factor * in_ref[h]


def shift(x, axis, by):
    n = lax.axis_size(axis)
    return lax.ppermute(x, axis, [(i, (i + by) % n) for i in range(n)])


def swap(x, axes):
    return lax.all_to_all(x, axes, 0, 0, tiled=True)


def body(queries, keys, values, out_grad, inputs, momentum, level_weight):
    length, width = queries.shape
    features = inputs.shape[1]
    n_y, n_z = lax.axis_size(Y), lax.axis_size(Z)
    heads = width // D
    sds = jax.ShapeDtypeStruct
    info = jnp.stack(
        [lax.axis_index(HEAD), lax.axis_index(Y), lax.axis_index(Z), jnp.int32(0)]
    ).astype(jnp.int32)

    square_sds = sds((length, width), bf16)
    held = pltpu.VMEM((length, width), bf16)
    dma = pltpu.SemaphoreType.DMA
    both = call(
        states_kernel,
        sds((heads, 2 * D, D), bf16),
        (queries, out_grad, keys, values),
        4 * length * width * D,
        [ANY] * 4,
        scratch=[held] * 4 + [dma((4,))],
        vmem=VMEM_ALL,
    )
    chunk = 512
    chunks = features // chunk
    keyed = call(
        local_kernel,
        tuple(sds((2, features, D), bf16) for _ in range(n_y)),
        (queries, keys, out_grad, inputs),
        4 * length * width * features + 3 * length * length * width,
        [ANY] * 4,
        (ANY,) * n_y,
        scratch=[held] * 3
        + [
            pltpu.VMEM((chunks, length, chunk), bf16),
            pltpu.VMEM((length, 2 * width), bf16),
            pltpu.VMEM((chunks, n_y, 2, chunk, D), bf16),
            dma((3 + chunks,)),
            dma((chunks, n_y)),
        ],
        scalars=(info, level_weight),
        vmem=52,
    )
    slices = (n_y * n_z, 2 * D // n_z, D)
    both = swap(both.reshape(slices), SEQ)
    gone = {n: shift(keyed[n], Y, n) for n in sorted(range(1, n_y), key=lambda n: abs(n - n_y // 2))}
    keyed = [keyed[0]] + [gone[n] for n in range(1, n_y)]

    both = call(
        tree_kernel,
        sds((n_z, n_y) + slices[1:], bf16),
        (both,),
        1 << 21,
        scalars=(info, level_weight),
        vmem=8,
    )
    both = swap(both, Z)

    rows = features // 2
    parts, *own = call(
        project_kernel,
        (sds((n_z, features // n_z, D), bf16),)
        + tuple(sds((n_z, 2 * D // n_z, D), bf16) for _ in range(n_y)),
        (*keyed, both),
        2 * features * n_y * D * D,
        [ANY] * (n_y + 1),
        (ANY,) * (n_y + 1),
        scratch=[
            pltpu.VMEM((2, n_y, 2, rows, D), bf16),
            pltpu.VMEM(both.shape, bf16),
            pltpu.VMEM((2, n_z, rows // n_z, D), bf16),
            dma((1,)),
            dma((2, n_y)),
            dma((2,)),
            dma((n_y,)),
        ],
        scalars=(info,),
        vmem=52,
    )
    parts = swap(parts, Z)

    own = [own[0]] + [shift(own[n], Y, n) for n in range(1, n_y)]
    query_grad, key_grad, value_grad, end = call(
        outputs_kernel,
        (sds((length, width), bf16),) * 3 + (sds((8, D), f32),),
        (queries, keys, values, out_grad, *own),
        6 * length * length * width,
        scalars=(info, level_weight),
        vmem=52,
    )

    near, rest = (Z,), HEAD + (Y,)
    rows = momentum.shape[0]
    square, shard = call(
        shard_kernel,
        (sds((lax.axis_size(near), 1, D), f32), sds((n_y, heads, rows, D), f32)),
        (parts,),
        1 << 20,
        scratch=[pltpu.VMEM((n_y * rows, D), f32)],
        scalars=(info,),
        after=(end,),
        vmem=8,
    )
    shard = lax.psum_scatter(
        shard.reshape(n_y * heads * rows, D), Y, scatter_dimension=0, tiled=True
    ).reshape(heads, rows, D)
    square = swap(square, near)
    total = call(
        stage_kernel, sds((lax.axis_size(rest), 1, D), f32), (square,), 1 << 16, vmem=8
    )
    total = swap(total, rest)
    new_momentum = call(
        final_kernel, sds(momentum.shape, f32), (momentum, shard, total), 1 << 16, vmem=8
    )
    return (query_grad, key_grad, value_grad, new_momentum)


def solution(mesh):
    torus = Mesh(mesh.devices.reshape(4, 2, 4, 16), HEAD + SEQ)
    tokens = P(SEQ, HEAD)
    return jax.shard_map(
        body,
        mesh=torus,
        in_specs=(tokens, tokens, tokens, tokens, P(SEQ, None), tokens, P()),
        out_specs=(tokens, tokens, tokens, tokens),
        check_vma=False,
    )
```

```python
import functools
import math

import jax
import jax.numpy as jnp
import numpy as np
from jax import lax
from jax.experimental import pallas as pl
from jax.experimental.pallas import tpu as pltpu
from jax.sharding import Mesh
from jax.sharding import PartitionSpec as P

D = 128
HEAD = ("head_0", "head_1")
Y = "seq_0"
Z = "seq_1"
SEQ = (Y, Z)

VMEM_ALL = 60

clip_norm = 1024.0
momentum_rate = 0.9

bf16 = jnp.bfloat16
f32 = jnp.float32


def dot(a, b, ca, cb):
    return lax.dot_general(a, b, (((ca,), (cb,)), ((), ())), preferred_element_type=f32)


VMEM = pl.BlockSpec(memory_space=pltpu.VMEM)
ANY = pl.BlockSpec(memory_space=pl.ANY)


def call(kernel, out_shape, operands, flops, in_specs=None, out_specs=None, grid=(), scratch=(), vmem=16, after=(), scalars=(), gated=()):
    leaves = jax.tree.leaves((operands, out_shape))
    n = len(scalars) + len(operands)
    skip = n + len(after) + len(gated)
    last = skip + len(jax.tree.leaves(out_shape))

    def run(*refs):
        kernel(*refs[:n], *refs[skip:last], *refs[last + len(gated) :])

    in_specs = list(in_specs or [None] * len(operands))
    in_specs = [VMEM if i is None else i for i in in_specs]
    if out_specs is None:
        out_specs = jax.tree.map(lambda _: VMEM, out_shape)
    anywhere = ANY
    aliases = {}
    if gated:
        first = len(jax.tree.leaves(out_shape))
        aliases = {n + len(after) + i: first + i for i in range(len(gated))}
        out_shape = (*jax.tree.leaves(out_shape), *(jax.ShapeDtypeStruct(x.shape, x.dtype) for x in gated))
        out_specs = (*jax.tree.leaves(out_specs), *(anywhere for _ in gated))
    return pl.pallas_call(
        run,
        out_shape=out_shape,
        grid_spec=pltpu.PrefetchScalarGridSpec(
            num_scalar_prefetch=len(scalars),
            grid=grid,
            in_specs=in_specs + [anywhere] * (len(after) + len(gated)),
            out_specs=out_specs,
            scratch_shapes=list(scratch),
        ),
        input_output_aliases=aliases,
        compiler_params=pltpu.CompilerParams(vmem_limit_bytes=vmem * 1024 * 1024),
        cost_estimate=pl.CostEstimate(
            flops=flops,
            bytes_accessed=sum(x.size * x.dtype.itemsize for x in leaves),
            transcendentals=0,
        ),
    )(*scalars, *operands, *after, *gated)


def lanes(block):
    if isinstance(block, int):
        return slice(block * D, (block + 1) * D)
    return pl.ds(pl.multiple_of(block * D, D), D)


def lam(level, head, weight_ref):
    factor = np.float32(2.0 ** (-0.5 * level) / (8.0 * math.sqrt(D)))
    return weight_ref[level, head].astype(f32) * factor


def diagonal(head, weight_ref, transposed):
    row = lax.broadcasted_iota(jnp.int32, (D, D), 0)
    col = lax.broadcasted_iota(jnp.int32, (D, D), 1)
    apart = jnp.bitwise_xor(row, col)
    out = jnp.full((D, D), lam(0, head, weight_ref), f32)
    for level in range(1, D.bit_length()):
        out = jnp.where(apart >= 1 << (level - 1), lam(level, head, weight_ref), out)
    keep = row <= col if transposed else col <= row
    return jnp.where(keep, out, f32(0.0))


def far(i, j, head, weight_ref):
    return lam(D.bit_length() - 1 + (i ^ j).bit_length(), head, weight_ref)


def weighted(scores, first, own, head, weight_ref, diag):
    count = scores.shape[1] // D
    parts = []
    for n in range(count):
        part = scores[:, n * D : (n + 1) * D]
        w = diag if first + n == own else far(first + n, own, head, weight_ref)
        parts.append((w * part).astype(bf16))
    return parts[0] if count == 1 else jnp.concatenate(parts, axis=1)


def start_all(pairs, sems):
    moves = [pltpu.make_async_copy(source, to, sems.at[i]) for i, (source, to) in enumerate(pairs)]
    for move in moves:
        move.start()
    return moves


def states_kernel(q_hbm, g_hbm, k_hbm, v_hbm, out_ref, q_ref, g_ref, k_ref, v_ref, sems):
    moves = start_all(
        [(q_hbm, q_ref), (g_hbm, g_ref), (k_hbm, k_ref), (v_hbm, v_ref)], sems
    )
    moves[0].wait()
    moves[1].wait()
    for h in range(out_ref.shape[0]):
        s = lanes(h)
        out_ref[h, :D, :] = dot(q_ref[:, s], g_ref[:, s], 0, 0).astype(bf16)
    moves[2].wait()
    moves[3].wait()
    for h in range(out_ref.shape[0]):
        s = lanes(h)
        out_ref[h, D:, :] = dot(k_ref[:, s], v_ref[:, s], 0, 0).astype(bf16)


def local_kernel(info_ref, weight_ref, q_hbm, k_hbm, g_hbm, x_hbm, *refs):
    out_hbm = refs[:-8]
    q_ref, k_ref, g_ref, x_ref, right_ref, done_ref, in_sems, out_sems = refs[-8:]
    n_y = len(out_hbm)
    chunks, _, chunk = x_ref.shape
    moves = start_all(
        [(k_hbm, k_ref), (q_hbm, q_ref), (g_hbm, g_ref)]
        + [(x_hbm.at[:, pl.ds(c * chunk, chunk)], x_ref.at[c]) for c in range(chunks)],
        in_sems,
    )
    for move in moves[:3]:
        move.wait()
    blocks = q_ref.shape[0] // D
    for n in range(n_y):
        h = lax.rem(info_ref[1] + n, n_y)
        s = lanes(h)
        head = info_ref[0] * n_y + h
        keys, query, grad = k_ref[:, s], q_ref[:, s], g_ref[:, s]
        right_ref[:, lanes(2 * n)] = keys
        diag = diagonal(head, weight_ref, True)
        for j in range(blocks):
            rows = slice(j * D, (j + 1) * D)
            scores = dot(keys[rows], query[j * D :], 1, 1)
            mixed = weighted(scores, j, j, head, weight_ref, diag)
            res = dot(mixed, grad[j * D :], 1, 0)
            right_ref[rows, lanes(2 * n + 1)] = res.astype(bf16)
    sent = []
    for c in range(chunks):
        moves[3 + c].wait()
        res = dot(x_ref[c], right_ref[...], 0, 0).astype(bf16)
        for n in range(n_y):
            done_ref[c, n, 0, :, :] = res[:, lanes(2 * n)]
            done_ref[c, n, 1, :, :] = res[:, lanes(2 * n + 1)]
        part = pl.ds(c * chunk, chunk)
        sent += start_all(
            [(done_ref.at[c, n], out_hbm[n].at[:, part, :]) for n in range(n_y)], out_sems.at[c]
        )
    for move in sent:
        move.wait()


def tree_kernel(info_ref, weight_ref, in_ref, out_ref):
    nz, ny = out_ref.shape[:2]
    count = in_ref.shape[0]
    depth = count.bit_length() - 1
    head = info_ref[0] * ny + info_ref[1]
    is_grad = info_ref[2] < nz // 2
    sums = [[in_ref[c].astype(f32) for c in range(count)]]
    for bit in range(depth - 1):
        last = sums[-1]
        sums.append([last[2 * b] + last[2 * b + 1] for b in range(len(last) // 2)])
    total = [jnp.zeros(in_ref.shape[1:], f32)]
    for bit in reversed(range(depth)):
        w = lam(D.bit_length() + 2 + bit, head, weight_ref)
        later = jnp.where(is_grad, w, f32(0.0))
        earlier = jnp.where(is_grad, f32(0.0), w)
        last = sums[bit]
        total = [
            total[b // 2] + (later * last[b + 1] if b % 2 == 0 else earlier * last[b - 1])
            for b in range(len(last))
        ]
    for c in range(count):
        out_ref[c % nz, c // nz] = total[c].astype(bf16)


def project_kernel(info_ref, a0, a1, a2, a3, r_hbm, out_hbm, *refs):
    own_hbm, a_ref, r_ref, zero_ref, done_ref, r_sem, a_sems, out_sems, own_sems = refs
    keyed = (a0, a1, a2, a3)
    n_y = len(keyed)
    chunks, _, _, rows, _ = a_ref.shape
    got = start_all([(r_hbm, r_ref)], r_sem)
    moves = []
    for c in range(chunks):
        part = pl.ds(c * rows, rows)
        moves.append(
            start_all(
                [(keyed[n].at[:, part, :], a_ref.at[c, n]) for n in range(n_y)], a_sems.at[c]
            )
        )
    y = info_ref[1]
    half = r_ref.shape[0] // 2
    nz = out_hbm.shape[0]
    each = out_hbm.shape[1] // n_y
    zero_ref[...] = jnp.zeros_like(zero_ref)
    got[0].wait()
    sent = []
    for d in range(n_y):
        sources = [r_ref.at[:, d]] + [zero_ref] * (n_y - 1)
        sent += start_all(
            [(x, own_hbm.at[d, lax.rem(y + n, n_y)]) for n, x in enumerate(sources)], own_sems.at[d]
        )
    states = [r_ref[:half, lax.rem(y + n_y - n, n_y)].reshape(D, D) for n in range(n_y)]
    states = jnp.concatenate(states, axis=0)
    for c in range(chunks):
        for move in moves[c]:
            move.wait()
        left = jnp.concatenate([a_ref[c, n, 0] for n in range(n_y)], axis=1)
        res = dot(left, states, 1, 0)
        for n in range(n_y):
            res = res + a_ref[c, n, 1].astype(f32)
        res = res.astype(bf16)
        inner = rows // (nz * each)
        for b in range(inner):
            for z in range(nz):
                done_ref[c, z, b * each : (b + 1) * each, :] = res[
                    (b * nz + z) * each : (b * nz + z + 1) * each, :
                ]
        sent += start_all(
            [(done_ref.at[c], out_hbm.at[:, pl.ds(c * inner * each, inner * each), :])],
            out_sems.at[pl.ds(c, 1)],
        )
    for move in sent:
        move.wait()


def outputs_kernel(
    info_ref, weight_ref, q_ref, k_ref, v_ref, g_ref, r_ref, dq_ref, dk_ref, dv_ref, end_ref
):
    n_y = r_ref.shape[0]
    end_ref[...] = jnp.zeros_like(end_ref)
    blocks = q_ref.shape[0] // D
    for h in range(n_y):
        s = lanes(h)
        head = info_ref[0] * n_y + h
        both = r_ref[h].reshape(2 * D, D)
        returned, carried = both[:D], both[D:]
        query, keys, values, grad = q_ref[:, s], k_ref[:, s], v_ref[:, s], g_ref[:, s]
        base_v = dot(keys, returned, 1, 0)
        base_k = dot(values, returned, 1, 1)
        base_q = dot(grad, carried, 1, 1)
        diag = diagonal(head, weight_ref, False)
        diag_t = diagonal(head, weight_ref, True)
        for i in range(blocks):
            rows = slice(i * D, (i + 1) * D)
            upto = (i + 1) * D
            before = dot(grad[rows], values[:upto], 1, 1)
            dmix = weighted(before, 0, i, head, weight_ref, diag)
            dq_ref[rows, s] = (base_q[rows] + dot(dmix, keys[:upto], 1, 0)).astype(bf16)
            later = dot(values[rows], grad[i * D :], 1, 1)
            dmix_t = weighted(later, i, i, head, weight_ref, diag_t)
            dk_ref[rows, s] = (base_k[rows] + dot(dmix_t, query[i * D :], 1, 0)).astype(bf16)
            scores = dot(keys[rows], query[i * D :], 1, 1)
            mixed_t = weighted(scores, i, i, head, weight_ref, diag_t)
            dv_ref[rows, s] = (base_v[rows] + dot(mixed_t, grad[i * D :], 1, 0)).astype(bf16)


def shard_kernel(info_ref, in_ref, square_ref, out_ref, total_ref):
    n_y, heads, rows = out_ref.shape[:3]
    total = in_ref[0].astype(f32)
    for z in range(1, in_ref.shape[0]):
        total = total + in_ref[z].astype(f32)
    total_ref[...] = total
    square = jnp.sum(jnp.sum(total * total, axis=0, keepdims=True), axis=1, keepdims=True)
    square_ref[...] = jnp.broadcast_to(square[None], square_ref.shape)
    out_ref[...] = jnp.zeros_like(out_ref)
    for y in range(n_y):
        out_ref[y, info_ref[1], :, :] = total_ref[y * rows : (y + 1) * rows, :]


def stage_kernel(square_ref, out_ref):
    square = jnp.sum(square_ref[...], axis=0, keepdims=True)
    out_ref[...] = jnp.broadcast_to(square, out_ref.shape)


def final_kernel(mom_ref, in_ref, total_ref, out_ref):
    total = jnp.sum(total_ref[...], axis=0)
    factor = jnp.minimum(f32(1.0), clip_norm / jnp.sqrt(total + 1e-06))
    for h in range(in_ref.shape[0]):
        s = lanes(h)
        out_ref[:, s] = momentum_rate * mom_ref[:, s] + factor * in_ref[h]


def shift(x, axis, by):
    n = lax.axis_size(axis)
    return lax.ppermute(x, axis, [(i, (i + by) % n) for i in range(n)])


def swap(x, axes):
    return lax.all_to_all(x, axes, 0, 0, tiled=True)


def body(queries, keys, values, out_grad, inputs, momentum, level_weight):
    length, width = queries.shape
    features = inputs.shape[1]
    n_y, n_z = lax.axis_size(Y), lax.axis_size(Z)
    heads = width // D
    sds = jax.ShapeDtypeStruct
    info = jnp.stack(
        [lax.axis_index(HEAD), lax.axis_index(Y), lax.axis_index(Z), jnp.int32(0)]
    ).astype(jnp.int32)

    square_sds = sds((length, width), bf16)
    held = pltpu.VMEM((length, width), bf16)
    dma = pltpu.SemaphoreType.DMA
    both = call(
        states_kernel,
        sds((heads, 2 * D, D), bf16),
        (queries, out_grad, keys, values),
        4 * length * width * D,
        [ANY] * 4,
        scratch=[held] * 4 + [dma((4,))],
        vmem=VMEM_ALL,
    )
    chunk = 512
    chunks = features // chunk
    keyed = call(
        local_kernel,
        tuple(sds((2, features, D), bf16) for _ in range(n_y)),
        (queries, keys, out_grad, inputs),
        4 * length * width * features + 3 * length * length * width,
        [ANY] * 4,
        (ANY,) * n_y,
        scratch=[held] * 3
        + [
            pltpu.VMEM((chunks, length, chunk), bf16),
            pltpu.VMEM((length, 2 * width), bf16),
            pltpu.VMEM((chunks, n_y, 2, chunk, D), bf16),
            dma((3 + chunks,)),
            dma((chunks, n_y)),
        ],
        scalars=(info, level_weight),
        vmem=52,
    )
    slices = (n_y * n_z, 2 * D // n_z, D)
    both = swap(both.reshape(slices), SEQ)
    gone = {n: shift(keyed[n], Y, n) for n in sorted(range(1, n_y), key=lambda n: abs(n - n_y // 2))}
    keyed = [keyed[0]] + [gone[n] for n in range(1, n_y)]

    both = call(
        tree_kernel,
        sds((n_z, n_y) + slices[1:], bf16),
        (both,),
        1 << 21,
        scalars=(info, level_weight),
        vmem=8,
    )
    both = swap(both, Z)

    rows = features // 2
    parts, own = call(
        project_kernel,
        (
            sds((n_z, features // n_z, D), bf16),
            sds((n_y, n_y, n_z, 2 * D // n_z, D), bf16),
        ),
        (*keyed, both),
        2 * features * n_y * D * D,
        [ANY] * (n_y + 1),
        (ANY,) * 2,
        scratch=[
            pltpu.VMEM((2, n_y, 2, rows, D), bf16),
            pltpu.VMEM(both.shape, bf16),
            pltpu.VMEM((n_z, 2 * D // n_z, D), bf16),
            pltpu.VMEM((2, n_z, rows // n_z, D), bf16),
            dma((1,)),
            dma((2, n_y)),
            dma((2,)),
            dma((n_y, n_y)),
        ],
        scalars=(info,),
        vmem=52,
    )
    parts = swap(parts, Z)

    own = lax.psum_scatter(own.reshape(n_y * n_y * 2 * D, D), Y, scatter_dimension=0, tiled=True)
    own = own.reshape(n_y, n_z, 2 * D // n_z, D)
    query_grad, key_grad, value_grad, end = call(
        outputs_kernel,
        (sds((length, width), bf16),) * 3 + (sds((8, D), f32),),
        (queries, keys, values, out_grad, own),
        6 * length * length * width,
        scalars=(info, level_weight),
        vmem=52,
    )

    near, rest = HEAD + (Y,), (Z,)
    rows = momentum.shape[0]
    square, shard = call(
        shard_kernel,
        (sds((lax.axis_size(near), 1, D), f32), sds((n_y, heads, rows, D), f32)),
        (parts,),
        1 << 20,
        scratch=[pltpu.VMEM((n_y * rows, D), f32)],
        scalars=(info,),
        vmem=8,
    )
    shard = lax.psum_scatter(
        shard.reshape(n_y * heads * rows, D), Y, scatter_dimension=0, tiled=True
    ).reshape(heads, rows, D)
    square = swap(square, near)
    total = call(
        stage_kernel,
        sds((lax.axis_size(rest), 1, D), f32),
        (square,),
        1 << 16,
        after=(end,),
        vmem=8,
    )
    total = swap(total, rest)
    new_momentum = call(
        final_kernel, sds(momentum.shape, f32), (momentum, shard, total), 1 << 16, vmem=8
    )
    return (query_grad, key_grad, value_grad, new_momentum)


def solution(mesh):
    torus = Mesh(mesh.devices.reshape(4, 2, 4, 16), HEAD + SEQ)
    tokens = P(SEQ, HEAD)
    return jax.shard_map(
        body,
        mesh=torus,
        in_specs=(tokens, tokens, tokens, tokens, P(SEQ, None), tokens, P()),
        out_specs=(tokens, tokens, tokens, tokens),
        check_vma=False,
    )
```
